512 devices in a mesh: leaf: 32 (over z, core), front: 16 (over x, y).
Axes of the slice: x: 4, y: 4, z: 16, core: 2. Of those that a mesh axis runs over, the one named last changes fastest.
Arguments:
- rhs: bfloat16 [4, 196608, 256], P(None, ('leaf', 'front')), may hold values from -6 to 6
- dinv: bfloat16 [4, 196608, 384], P(None, ('leaf', 'front'))
- u_factor: bfloat16 [3, 196608, 128], P(None, ('leaf', 'front')), may hold values from -0.5 to 0.5
- v_factor: bfloat16 [3, 196608, 128], P(None, ('leaf', 'front')), may hold values from -0.02734375 to 0.02734375
- rank_sizes: int32 [3], replicated, may hold values from 64 to 128, as said below
- resid: float32 [32768, 256], P(('leaf', 'front')), may hold values from -6 to 6
- dest_front: int32 [32768, 1], P(('leaf', 'front')), may hold values from 0 to 15; in each aligned block of 64 rows (0 to 63, 64 to 127, ...) at most 8 rows name the same one
- dest_row: int32 [32768], P(('leaf', 'front')), may hold values from 0 to 383
- live_count: int32 [512], P(('leaf', 'front')), may hold values from 32 to 64, as said below
Outputs:
- solved: float32 [4, 196608, 256], P(None, ('leaf', 'front'))
The draws below stay inside these ranges and needn't reach their ends.
Inputs may be any that keep to these rules, and one draw needn't show every extreme that they name: `rank_sizes`: each coupling's rank is at most 128, and some coupling has rank 128. `live_count`: some device has all 64 slots live. `dest_front`: among the slots of one device at most 8 name the same front index, live or not.
All inputs are finite; a program needn't handle non-finite values.
Results may differ from the reference program's by a relative error of at most 0.0003.
Values sent between devices are 32-bit elements; how exact they have to be, the bound alone decides.
No kernel may reach another device: no remote copies, remote signals or barrier semaphores. Data moves between devices by JAX's collectives and lax.ppermute only.
A program may use at most 64 MiB of HBM per device.

```python
import math
import jax
import jax.numpy as jnp
import numpy as np
from jax import lax

RHS = 256
RANK = 128
LEVELS = 4
SEP_DEV = 384
REC_DEV = 64
FRONT_DEVS = 16
ROWS = 196608
RECS = 32768
CAP = 8


def draw_dinv(key, part):
    key = jax.random.fold_in(key, 11)
    first_key, second_key = jax.random.split(key)
    shape = (LEVELS, ROWS, SEP_DEV)
    spread = 0.45 / SEP_DEV ** 0.5
    off_part = jax.random.normal(first_key, shape, jnp.float32) * spread
    diag_part = jax.random.uniform(second_key, shape, jnp.float32, 0.8, 1.2)
    on_diag = jnp.arange(ROWS)[:, None] % SEP_DEV == jnp.arange(SEP_DEV)[None, :]
    return jnp.where(on_diag[None, :, :], diag_part, off_part).astype(jnp.bfloat16)


def draw_rank_sizes(key, part):
    key = jax.random.fold_in(key, 12)
    first_key, second_key = jax.random.split(key)
    values = jax.random.randint(first_key, (LEVELS - 1,), RANK // 2, RANK + 1)
    chosen = jax.random.randint(second_key, (), 0, LEVELS - 1)
    return jnp.where(jnp.arange(LEVELS - 1) == chosen, RANK, values).astype(jnp.int32)


def draw_live_count(key, part):
    key = jax.random.fold_in(key, 13)
    first_key, second_key = jax.random.split(key)
    device_count = RECS // REC_DEV
    values = jax.random.randint(first_key, (device_count,), REC_DEV // 2, REC_DEV + 1)
    chosen = jax.random.randint(second_key, (), 0, device_count)
    return jnp.where(jnp.arange(device_count) == chosen, REC_DEV, values).astype(jnp.int32)


def with_ends(array, key, low, largest):
    longest = array.shape.index(max(array.shape))
    spots = []
    for shift in (0, 1):
        where = [jax.random.randint(jax.random.fold_in(key, axis), (), 0, length) for axis, length in enumerate(array.shape)]
        where[longest] = (where[longest] + shift) % array.shape[longest]
        spots.append(tuple(where))
    return array.at[spots[0]].set(low).at[spots[1]].set(largest)


def steps_of(stream_key, dims, cuts, smallest, top_value):
    factor_of, own = 1.0, jax.random.fold_in(stream_key, 6)
    for axis_at, shards_of in cuts:
        draws = jnp.exp(jax.random.uniform(jax.random.fold_in(own, axis_at), (shards_of,), jnp.float32, smallest / len(cuts), top_value / len(cuts)))
        factor_of = factor_of * jnp.repeat(draws, dims[axis_at] // shards_of).reshape([-1 if axis == axis_at else 1 for axis in range(len(dims))])
    return factor_of


def deal_out(key, own, number, rows, number_of, top, limit, skew):
    sequence = jax.random.permutation(key, number_of)
    crowded, ordinary = portions_of(number_of, rows * top, limit, skew, True), portions_of(number_of, rows * top, limit, skew, False)
    places = jnp.arange(number_of)

    def named(tallies, rotation):
        used = int((tallies > 0).sum())
        fixed = max(1, used // 4)
        shifted = fixed + (places - fixed + rotation * (used - fixed)) % max(1, number_of - fixed)
        return jnp.zeros((number_of,), jnp.int32).at[sequence[jnp.where(places < fixed, places, shifted)]].set(jnp.asarray(tallies, jnp.int32))

    tallies = jnp.where(number % 4 == 0, named(crowded, number // 4), named(ordinary, number - number // 4 - 1))
    mixed = jax.random.permutation(jax.random.fold_in(own, 3), number_of)
    donor, receiver = mixed[0:number_of // 2 * 2:2], mixed[1:number_of // 2 * 2:2]
    room = jnp.minimum(tallies[donor] - 1, limit - tallies[receiver]) // 2
    room = jnp.where((donor == sequence[0]) | (receiver == sequence[0]) | (tallies[receiver] == 0), 0, jnp.maximum(room, 0))
    shifted = jax.random.randint(jax.random.fold_in(own, 4), (number_of // 2,), 0, 1 << 20) % (room + 1)
    tallies = tallies.at[donor].add(-shifted).at[receiver].add(shifted)
    items = jnp.searchsorted(jnp.cumsum(tallies), jnp.arange(rows * top), side="right").astype(jnp.int32)
    table = items.reshape(top, rows).T
    table = table[jax.random.permutation(jax.random.fold_in(own, 1), rows)]
    rotation = jax.random.randint(jax.random.fold_in(own, 2), (rows, 1), 0, top)
    return jnp.take_along_axis(table, (jnp.arange(top)[None, :] + rotation) % top, axis=1)


def portions_of(number_of, total, reach, lean, full):
    loads = [(1 << 20) // math.isqrt(grade ** lean) + 1 for grade in range(1, number_of + 1)]
    largest = reach if full else min(reach, max(-(-total // number_of), total * loads[0] // sum(loads)))
    least = 1 if total - largest >= number_of - 1 else 0
    counts, spare = [largest] + [least] * (number_of - 1), total - largest - least * (number_of - 1)
    while spare > 0:
        free = [i for i in range(1, number_of) if counts[i] < largest] or [i for i in range(1, number_of) if counts[i] < reach]
        mass, left = sum([loads[i] for i in free]), spare
        for i in free:
            extra = min(reach - counts[i], max(1, left * loads[i] // mass), spare)
            counts[i] = counts[i] + extra
            spare = spare - extra
    return np.array(counts)


def noise(key, shape, scale, limit, cuts=(), kind=jnp.bfloat16):
    array = scale * jax.random.normal(key, shape, jnp.float32)
    if cuts:
        array = array * steps_of(key, shape, cuts, -0.22, 0.18)
    return jnp.clip(array, -limit, limit).astype(kind)


def setup_inputs(seed: int = 0) -> dict:
    key_of = jax.random.split(jax.random.key(seed), 10)
    rhs = noise(key_of[0], (LEVELS, ROWS, RHS), 1.0, 6.0, ((1, 512),))
    dinv = draw_dinv(jax.random.fold_in(key_of[9], 71), 0)
    u_factor = noise(key_of[2], (LEVELS - 1, ROWS, RANK), RANK ** -0.5, 0.5, ((1, 512),))
    v_factor = noise(key_of[3], (LEVELS - 1, ROWS, RANK), (ROWS // 4) ** -0.5, 0.02734375, ((1, 512),))
    rank_sizes = draw_rank_sizes(jax.random.fold_in(key_of[9], 71), 0)
    resid = noise(key_of[5], (RECS, RHS), 1.0, 6.0, ((0, 512),), jnp.float32)
    dest_front_keys = jax.random.split(jax.random.fold_in(key_of[6], 1), RECS // REC_DEV)
    dest_front_turns = jax.random.permutation(jax.random.fold_in(key_of[6], 3), RECS // REC_DEV)
    dest_front = jax.vmap(lambda own, number: deal_out(jax.random.fold_in(key_of[6], 2), own, number, REC_DEV, FRONT_DEVS, 1, CAP, 1))(dest_front_keys, dest_front_turns).reshape((RECS, 1))
    dest_row = with_ends(jax.random.randint(key_of[7], (RECS,), 0, SEP_DEV), jax.random.fold_in(key_of[7], 1), 0, SEP_DEV - 1).astype(jnp.int32)
    live_count = draw_live_count(jax.random.fold_in(key_of[9], 71), 0)
    return dict(rhs=rhs, dinv=dinv, u_factor=u_factor, v_factor=v_factor, rank_sizes=rank_sizes, resid=resid, dest_front=dest_front, dest_row=dest_row, live_count=live_count)


def apply_block(block_level, vector_field):
    blocks = block_level.astype(jnp.float32).reshape(-1, SEP_DEV, SEP_DEV)
    pieces = vector_field.reshape(-1, SEP_DEV, RHS)
    result = jnp.einsum("dij,djr->dir", blocks, pieces, precision=lax.Precision.HIGHEST)
    return result.reshape(-1, RHS)


def rank_space(factor, vector_field, node_count):
    factor_nodes = factor.astype(jnp.float32).reshape(node_count, -1, RANK)
    field_nodes = vector_field.reshape(node_count, -1, RHS)
    return jnp.einsum("nir,nic->nrc", factor_nodes, field_nodes, precision=lax.Precision.HIGHEST)


def expand_rank(factor, coupled, node_count):
    factor_nodes = factor.astype(jnp.float32).reshape(node_count, -1, RANK)
    result = jnp.einsum("nir,nrc->nic", factor_nodes, coupled, precision=lax.Precision.HIGHEST)
    return result.reshape(-1, RHS)


def reference(rhs, dinv, u_factor, v_factor, rank_sizes, resid, dest_front, dest_row, live_count):
    total_rows = rhs.shape[1]
    slots = jnp.arange(RECS, dtype=jnp.int32)
    owner = slots // REC_DEV
    live_slots = (slots % REC_DEV) < live_count[owner]
    target = (owner // FRONT_DEVS) * FRONT_DEVS + dest_front[:, 0]
    row_ids = (target * SEP_DEV + dest_row).astype(jnp.int32)
    values = jnp.where(live_slots[:, None], resid, jnp.zeros_like(resid))
    sources = jax.ops.segment_sum(values, row_ids, num_segments=total_rows)
    forward = [None] * LEVELS
    forward[LEVELS - 1] = apply_block(dinv[LEVELS - 1], rhs[LEVELS - 1].astype(jnp.float32) + sources)
    masks = []
    for coupling in range(LEVELS - 1):
        masks.append((jnp.arange(RANK) < rank_sizes[coupling]).astype(jnp.float32)[None, :, None])
    for coupling in range(LEVELS - 2, -1, -1):
        node_count = 2 ** coupling
        coupled = rank_space(v_factor[coupling], forward[coupling + 1], node_count) * masks[coupling]
        reduced = rhs[coupling].astype(jnp.float32) - expand_rank(u_factor[coupling], coupled, node_count)
        forward[coupling] = apply_block(dinv[coupling], reduced)
    solved = [forward[0]]
    for coupling in range(LEVELS - 1):
        node_count = 2 ** coupling
        dual = rank_space(u_factor[coupling], solved[coupling], node_count) * masks[coupling]
        update = apply_block(dinv[coupling + 1], expand_rank(v_factor[coupling], dual, node_count))
        solved.append(forward[coupling + 1] - update)
    return jnp.stack(solved)
```

```python
import functools

import jax
import jax.numpy as jnp
from jax import lax
from jax.experimental import pallas as pl
from jax.experimental.pallas import tpu as pltpu
from jax.sharding import Mesh
from jax.sharding import PartitionSpec as P

F32 = jnp.float32
BF16 = jnp.bfloat16
LEVELS = 4
RANK = 128
SHOTS = 256
ROWS = 384
SLOTS = 8
FRONT = 16
HALF = RANK // 2
PART = 18
EARLY = 4 * PART
MESSAGE = EARLY + 16
SENT = 24
SPREAD = 32
ALL = ("zh", "zl", "core", "x", "y")

A2, R1V, A1, R0V, S0, B0, S1, B1, C1, S2, B2, C2, R2V = 0, 1, 3, 4, 6, 8, 9, 11, 12, 13, 15, 16, 17
G_R2V, G_A2, G_R1V, G_A1, G_R0V, G_S0, G_B0, G_S1, G_B1, G_C1, G_S2, G_B2, G_C2 = (
    0, 8, 12, 16, 18, 20, 22, 23, 25, 26, 27, 29, 30,
)


SOLVE = 16
BOTTOM = 53
WHOLE = 62


def params(mebibytes):
    return pltpu.CompilerParams(vmem_limit_bytes=int(mebibytes * 2**20))


VMEM = pl.BlockSpec(memory_space=pltpu.VMEM)
SMEM = pl.BlockSpec(memory_space=pltpu.SMEM)
HBM = pl.BlockSpec(memory_space=pltpu.HBM)


def split(value):
    high = value.astype(BF16)
    return high, (value - high.astype(F32)).astype(BF16)


def split3(value):
    high = value.astype(BF16)
    rest = value - high.astype(F32)
    mid = rest.astype(BF16)
    return high, mid, (rest - mid.astype(F32)).astype(BF16)


def mm(left, right):
    return jnp.dot(left, right, preferred_element_type=F32)


def mm_tn(left, right):
    return lax.dot_general(left, right, (((0,), (0,)), ((), ())), preferred_element_type=F32)


def mm_nt(left, right):
    return lax.dot_general(left, right, (((1,), (1,)), ((), ())), preferred_element_type=F32)


def mm3(left, right):
    left_high, left_low = split(left)
    right_high, right_low = split(right)
    return mm(left_high, right_high) + (mm(left_high, right_low) + mm(left_low, right_high))


def column(row_ref, count):
    diagonal = lax.broadcasted_iota(jnp.int32, (count, count), 0) == lax.broadcasted_iota(
        jnp.int32, (count, count), 1
    )
    return jnp.sum(jnp.where(diagonal, row_ref[...], 0), axis=1, keepdims=True)


def pack_kernel(
    core_ref, live_ref, resid_hbm, front_hbm, row_hbm, out_ref, core_out,
    resid_ref, front_ref, row_ref, sems,
):
    core_out[0] = core_ref[0]
    copies = [
        pltpu.make_async_copy(source, target, sems.at[index])
        for index, (source, target) in enumerate(
            ((front_hbm, front_ref), (row_hbm, row_ref), (resid_hbm, resid_ref))
        )
    ]
    for copy in copies:
        copy.start()
    recv = resid_ref.shape[0]
    live = lax.broadcasted_iota(jnp.int32, (recv, 1), 0) < live_ref[0]
    copies[0].wait()
    front = column(front_ref, recv)
    copies[1].wait()
    rows = jnp.where(live, column(row_ref, recv) + 1, 0)
    onehot = front == lax.broadcasted_iota(jnp.int32, (recv, FRONT), 1)
    earlier = lax.broadcasted_iota(jnp.int32, (recv, recv), 0) > lax.broadcasted_iota(
        jnp.int32, (recv, recv), 1
    )
    before = mm(earlier.astype(F32).astype(BF16), onehot.astype(F32).astype(BF16))
    position = jnp.sum(jnp.where(onehot, before, 0.0), axis=1, keepdims=True)
    slot = front * SLOTS + position.astype(jnp.int32)
    place = slot == lax.broadcasted_iota(jnp.int32, (recv, FRONT * SLOTS), 1)
    place = place.astype(F32).astype(BF16)
    copies[2].wait()
    high, mid, low = split3(jnp.where(live, resid_ref[...], 0.0))
    coarse = jnp.broadcast_to((rows & ~15).astype(F32), (recv, 128)).astype(BF16)
    fine = jnp.broadcast_to((rows & 15).astype(F32), (recv, 128)).astype(BF16)
    out_ref[:, :SHOTS] = mm_tn(place, high) + (mm_tn(place, mid) + mm_tn(place, low))
    out_ref[:, SHOTS:] = mm_tn(place, coarse) + mm_tn(place, fine)


def local_kernel(
    core_ref, rhs_hbm, dinv_hbm, u_hbm, v_hbm,
    own_hbm, bottom_hbm, up_hbm, down_hbm, mine_ref, send_ref,
    rhs_ref, dinv_ref, u_ref, v_ref, own_ref, up_ref, down_ref, wide_ref, narrow_ref,
    in_sems, out_sems,
):
    core = core_ref[0]
    loads = []
    for level in range(LEVELS):
        pairs = [(dinv_hbm, dinv_ref), (rhs_hbm, rhs_ref)]
        if level < LEVELS - 1:
            pairs += [(u_hbm, u_ref), (v_hbm, v_ref)]
        loads.append(
            [
                pltpu.make_async_copy(source.at[level], target.at[level], in_sems.at[level, index])
                for index, (source, target) in enumerate(pairs)
            ]
        )
        for copy in loads[-1]:
            copy.start()
    stores = []

    def keep(source, target):
        copy = pltpu.make_async_copy(source, target, out_sems.at[len(stores)])
        copy.start()
        stores.append(copy)

    def reduce(factor, pair):
        return mm_tn(factor, pair[0]) + mm_tn(factor, pair[1])

    def save(at, value):
        scratch = narrow_ref if value.shape[1] == 128 else wide_ref
        scratch[...] = value
        for piece in range(value.shape[1] // 128):
            rows = pl.ds(at + piece, HALF, stride=PART)
            lanes = slice(piece * 128, piece * 128 + 128)
            mine_ref[rows, :] = scratch[pl.ds(core * HALF, HALF), lanes]
            send_ref[rows, :] = scratch[pl.ds((1 - core) * HALF, HALF), lanes]

    mine_ref[...] = jnp.zeros_like(mine_ref)
    send_ref[...] = jnp.zeros_like(send_ref)
    for level in range(LEVELS):
        for copy in loads[level]:
            copy.wait()
        block = dinv_ref[level]
        own = mm(block, rhs_ref[level])
        own_ref[level] = own
        keep(own_ref.at[level], own_hbm.at[level] if level < LEVELS - 1 else bottom_hbm)
        if level > 0:
            down = split(mm(block, v_ref[level - 1]))
            down_ref[level - 1, 0], down_ref[level - 1, 1] = down
            keep(down_ref.at[level - 1], down_hbm.at[level - 1])
        if level == LEVELS - 1:
            continue
        up = split(mm(block, u_ref[level]))
        up_ref[level, 0], up_ref[level, 1] = up
        keep(up_ref.at[level], up_hbm.at[level])
        own = split(own)
        save((S0, S1, S2)[level], reduce(u_ref[level], own))
        save((B0, B1, B2)[level], reduce(u_ref[level], up))
        if level > 0:
            save((None, R0V, R1V)[level], reduce(v_ref[level - 1], own))
            save((None, A1, A2)[level], reduce(v_ref[level - 1], up))
            save((None, C1, C2)[level], reduce(u_ref[level], down))
    for copy in stores:
        copy.wait()


def bottom_kernel(
    got_ref, dinv_hbm, v_hbm, own_hbm, forward_ref, coupled_ref, dinv_ref, v_ref, own_ref, sems
):
    copies = [
        pltpu.make_async_copy(source, target, sems.at[index])
        for index, (source, target) in enumerate(
            (
                (dinv_hbm.at[LEVELS - 1], dinv_ref),
                (own_hbm, own_ref),
                (v_hbm.at[LEVELS - 2], v_ref),
            )
        )
    ]
    for copy in copies:
        copy.start()
    rowid = got_ref[:, SHOTS:]
    lane = lax.broadcasted_iota(jnp.int32, rowid.shape, 1).astype(F32) + 1.0
    select = jnp.concatenate(
        [(rowid == lane + 128.0 * part).astype(F32).astype(BF16) for part in range(ROWS // 128)],
        axis=1,
    )
    high, mid, low = split3(got_ref[:, :SHOTS])
    copies[0].wait()
    chosen = mm_nt(dinv_ref[...], select).astype(BF16)
    copies[1].wait()
    forward = own_ref[...] + (mm(chosen, high) + (mm(chosen, mid) + mm(chosen, low)))
    forward_ref[...] = forward
    high, low = split(forward)
    copies[2].wait()
    coupled_ref[...] = mm_tn(v_ref[...], high) + mm_tn(v_ref[...], low)


def message_kernel(coupled_ref, mine_ref, other_ref, out_ref):
    for front in range(FRONT):
        early = slice(front * EARLY, front * EARLY + EARLY)
        base = front * MESSAGE
        out_ref[base : base + EARLY, :] = mine_ref[early, :] + other_ref[early, :]
        for half in range(2):
            rows = slice(half * HALF + 4 * front, half * HALF + 4 * front + 4)
            for piece in range(2):
                at = base + EARLY + half * 8 + piece * 4
                out_ref[at : at + 4, :] = coupled_ref[rows, piece * 128 : piece * 128 + 128]


def total_kernel(core_ref, pieces_ref, out_ref):
    core = core_ref[0]
    total = pieces_ref[0]
    for index in range(1, FRONT):
        total = total + pieces_ref[index]
    out_ref[...] = jnp.zeros_like(out_ref)
    for zl in range(4):
        out_ref[zl * 2 + core, :R2V] = total[zl * PART : zl * PART + R2V]
        for half in range(2):
            for piece in range(2):
                at = EARLY + half * 8 + piece * 4 + zl
                out_ref[zl * 2 + half, R2V + piece : R2V + piece + 1] = total[at : at + 1]


def nodes_kernel(zh_ref, cross_ref, out_ref):
    zh = zh_ref[0]
    order = [zh, zh ^ 1, zh ^ 2, zh ^ 3]
    out_ref[...] = jnp.zeros_like(out_ref)
    for zl in range(4):
        nodes = [cross_ref[node * 4 + zl] for node in order]
        pair, other = nodes[0] + nodes[1], nodes[2] + nodes[3]
        total = pair + other
        for index, node in enumerate(nodes):
            out_ref[zl, G_R2V + 2 * index : G_R2V + 2 * index + 2] = node[R2V : R2V + 2]
            out_ref[zl, G_A2 + index : G_A2 + index + 1] = node[A2 : A2 + 1]
        for index, value in enumerate((pair, other)):
            out_ref[zl, G_R1V + 2 * index : G_R1V + 2 * index + 2] = value[R1V : R1V + 2]
            out_ref[zl, G_A1 + index : G_A1 + index + 1] = value[A1 : A1 + 1]
        out_ref[zl, G_R0V : G_R0V + 5] = total[R0V : R0V + 5]
        out_ref[zl, G_S1 : G_S1 + 4] = pair[S1 : S1 + 4]
        out_ref[zl, G_S2 : G_S2 + 4] = nodes[0][S2 : S2 + 4]


def solve_kernel(
    core_ref, rank_ref, mine_ref, other_ref, own_ref, forward_ref, up_ref, down_ref, out_hbm,
    out_ref, out_sems,
):
    stores = []

    def finish(level, value):
        out_ref[level] = value
        copy = pltpu.make_async_copy(out_ref.at[level], out_hbm.at[level], out_sems.at[level])
        copy.start()
        stores.append(copy)

    first = core_ref[0] == 0

    def block(at):
        mine = mine_ref[pl.ds(at, HALF, stride=SPREAD), :]
        other = other_ref[pl.ds(at, HALF, stride=SPREAD), :]
        return jnp.concatenate(
            [jnp.where(first, mine, other), jnp.where(first, other, mine)], axis=0
        )

    def wide(at):
        return jnp.concatenate([block(at), block(at + 1)], axis=1)

    def mask(coupling, value):
        keep = lax.broadcasted_iota(jnp.int32, value.shape, 0) < rank_ref[coupling]
        return jnp.where(keep, value, 0.0)

    def expand(pair_ref, index, value):
        high, low = split(value)
        left_high, left_low = pair_ref[index, 0], pair_ref[index, 1]
        return mm(left_high, high) + (mm(left_high, low) + mm(left_low, high))

    c2 = [mask(2, wide(G_R2V + 2 * node)) for node in range(4)]
    t1 = [mm3(block(G_A2 + node), c2[node]) for node in range(4)]
    c1 = [mask(1, wide(G_R1V + 2 * half) - (t1[2 * half] + t1[2 * half + 1])) for half in range(2)]
    t0 = [mm3(block(G_A1 + half), c1[half]) for half in range(2)]
    c0 = mask(0, wide(G_R0V) - (t0[0] + t0[1]))
    d0 = mask(0, wide(G_S0) - mm3(block(G_B0), c0))
    d1 = mask(1, wide(G_S1) - mm3(block(G_B1), c1[0]) - mm3(block(G_C1), d0))
    d2 = mask(2, wide(G_S2) - mm3(block(G_B2), c2[0]) - mm3(block(G_C2), d1))
    finish(0, own_ref[0] - expand(up_ref, 0, c0))
    finish(1, own_ref[1] - expand(up_ref, 1, c1[0]) - expand(down_ref, 0, d0))
    finish(2, own_ref[2] - expand(up_ref, 2, c2[0]) - expand(down_ref, 1, d1))
    finish(3, forward_ref[...] - expand(down_ref, 2, d2))
    for copy in stores:
        copy.wait()


def per_device(rhs, dinv, u_factor, v_factor, rank_sizes, resid, dest_front, dest_row, live_count):
    core = lax.axis_index("core").astype(jnp.int32).reshape(1)
    zh = lax.axis_index("zh").astype(jnp.int32).reshape(1)

    front = ("x", "y")
    swap = [(0, 1), (1, 0)]

    packed, core_after = pl.pallas_call(
        pack_kernel,
        out_shape=(
            jax.ShapeDtypeStruct((FRONT * SLOTS, SHOTS + 128), F32),
            jax.ShapeDtypeStruct((1,), jnp.int32),
        ),
        in_specs=[SMEM, SMEM, HBM, HBM, HBM],
        out_specs=(VMEM, SMEM),
        scratch_shapes=[
            pltpu.VMEM(resid.shape, F32),
            pltpu.VMEM((1, resid.shape[0]), jnp.int32),
            pltpu.VMEM((1, resid.shape[0]), jnp.int32),
            pltpu.SemaphoreType.DMA((3,)),
        ],
        compiler_params=params(WHOLE),
    )(core, live_count, resid, dest_front.reshape(1, -1), dest_row.reshape(1, -1))
    got = lax.all_to_all(
        packed.reshape(FRONT, SLOTS, SHOTS + 128), front, 0, 0, tiled=True
    ).reshape(FRONT * SLOTS, SHOTS + 128)

    pair = jax.ShapeDtypeStruct((LEVELS - 1, 2, ROWS, RANK), BF16)
    early = jax.ShapeDtypeStruct((HALF * PART, 128), F32)
    own, bottom, up, down, mine, send = pl.pallas_call(
        local_kernel,
        out_shape=(
            jax.ShapeDtypeStruct((LEVELS - 1, ROWS, SHOTS), F32),
            jax.ShapeDtypeStruct((ROWS, SHOTS), F32),
            pair,
            pair,
            early,
            early,
        ),
        in_specs=[SMEM] + [HBM] * 4,
        out_specs=(HBM,) * 4 + (VMEM,) * 2,
        scratch_shapes=[
            pltpu.VMEM(rhs.shape, BF16),
            pltpu.VMEM(dinv.shape, BF16),
            pltpu.VMEM(u_factor.shape, BF16),
            pltpu.VMEM(v_factor.shape, BF16),
            pltpu.VMEM((LEVELS, ROWS, SHOTS), F32),
            pltpu.VMEM(pair.shape, BF16),
            pltpu.VMEM(pair.shape, BF16),
            pltpu.VMEM((RANK, SHOTS), F32),
            pltpu.VMEM((RANK, RANK), F32),
            pltpu.SemaphoreType.DMA((LEVELS, 4)),
            pltpu.SemaphoreType.DMA((10,)),
        ],
        compiler_params=params(WHOLE),
        cost_estimate=pl.CostEstimate(
            flops=2_000_000_000, bytes_accessed=8_000_000, transcendentals=0
        ),
    )(core_after, rhs, dinv, u_factor, v_factor)
    got, send = lax.optimization_barrier((got, send))
    other = lax.ppermute(send, "core", swap)

    forward, coupled = pl.pallas_call(
        bottom_kernel,
        out_shape=(
            jax.ShapeDtypeStruct((ROWS, SHOTS), F32),
            jax.ShapeDtypeStruct((RANK, SHOTS), F32),
        ),
        in_specs=[VMEM] + [HBM] * 3,
        out_specs=(VMEM, VMEM),
        scratch_shapes=[
            pltpu.VMEM((ROWS, ROWS), BF16),
            pltpu.VMEM((ROWS, RANK), BF16),
            pltpu.VMEM((ROWS, SHOTS), F32),
            pltpu.SemaphoreType.DMA((3,)),
        ],
        compiler_params=params(BOTTOM),
    )(got, dinv, v_factor, bottom)
    message = pl.pallas_call(
        message_kernel,
        out_shape=jax.ShapeDtypeStruct((FRONT * MESSAGE, 128), F32),
        in_specs=[VMEM] * 3,
        out_specs=VMEM,
        compiler_params=params(4),
    )(coupled, mine, other)
    pieces = lax.all_to_all(message.reshape(FRONT, MESSAGE, 128), front, 0, 0, tiled=True)
    summed = pl.pallas_call(
        total_kernel,
        out_shape=jax.ShapeDtypeStruct((8, SENT, 128), F32),
        in_specs=[SMEM, VMEM],
        out_specs=VMEM,
        compiler_params=params(4),
    )(core, pieces)
    pieces = lax.all_to_all(summed, ("zl", "core"), 0, 0, tiled=True)
    reduced = jnp.sum(pieces, axis=0, keepdims=True)
    cross = lax.all_to_all(
        jnp.broadcast_to(reduced, (16, SENT, 128)), ("zh", "zl"), 0, 0, tiled=True
    )
    spread = pl.pallas_call(
        nodes_kernel,
        out_shape=jax.ShapeDtypeStruct((4, SPREAD, 128), F32),
        in_specs=[SMEM, VMEM],
        out_specs=VMEM,
        compiler_params=params(4),
    )(zh, cross)
    gathered = lax.all_to_all(
        jnp.broadcast_to(spread.reshape(1, 4 * SPREAD, 128), (FRONT, 4 * SPREAD, 128)),
        front, 0, 0, tiled=True,
    ).reshape(HALF * SPREAD, 128)
    other = lax.ppermute(gathered, "core", swap)

    return pl.pallas_call(
        solve_kernel,
        out_shape=jax.ShapeDtypeStruct((LEVELS, ROWS, SHOTS), F32),
        in_specs=[SMEM] * 2 + [VMEM] * 6,
        out_specs=HBM,
        scratch_shapes=[
            pltpu.VMEM((LEVELS, ROWS, SHOTS), F32),
            pltpu.SemaphoreType.DMA((LEVELS,)),
        ],
        compiler_params=params(SOLVE),
    )(core, rank_sizes, gathered, other, own, forward, up, down)


def solution(mesh):
    grid = Mesh(mesh.devices.reshape(4, 4, 2, 4, 4), ALL)
    wide = P(None, ALL, None)
    return jax.shard_map(
        per_device,
        mesh=grid,
        in_specs=(wide, wide, wide, wide, P(), P(ALL, None), P(ALL, None), P(ALL), P(ALL)),
        out_specs=wide,
        check_vma=False,
    )
```

```python
import functools

import jax
import jax.numpy as jnp
from jax import lax
from jax.experimental import pallas as pl
from jax.experimental.pallas import tpu as pltpu
from jax.sharding import Mesh
from jax.sharding import PartitionSpec as P

F32 = jnp.float32
BF16 = jnp.bfloat16
LEVELS = 4
RANK = 128
SHOTS = 256
ROWS = 384
SLOTS = 8
FRONT = 16
HALF = RANK // 2
PART = 18
EARLY = 4 * PART
MESSAGE = EARLY + 16
SENT = 32
CROSS = 16
NODE = 4
SPREAD = 32
ALL = ("zh", "zl", "core", "x", "y")

A2, R1V, A1, R0V, S0, B0, S1, B1, C1, S2, B2, C2 = 0, 1, 3, 4, 6, 8, 9, 11, 12, 13, 15, 16
R2V = S2
G_R2V, G_A2, G_R1V, G_A1, G_R0V, G_S0, G_B0, G_S1, G_B1, G_C1, G_S2, G_B2, G_C2 = (
    0, 8, 12, 16, 18, 20, 22, 23, 25, 26, 27, 29, 30,
)


SOLVE = 16
WHOLE = 62


def params(mebibytes):
    return pltpu.CompilerParams(vmem_limit_bytes=int(mebibytes * 2**20))


VMEM = pl.BlockSpec(memory_space=pltpu.VMEM)
SMEM = pl.BlockSpec(memory_space=pltpu.SMEM)
HBM = pl.BlockSpec(memory_space=pltpu.HBM)


def split(value):
    high = value.astype(BF16)
    return high, (value - high.astype(F32)).astype(BF16)


def split3(value):
    high = value.astype(BF16)
    rest = value - high.astype(F32)
    mid = rest.astype(BF16)
    return high, mid, (rest - mid.astype(F32)).astype(BF16)


def mm(left, right):
    return jnp.dot(left, right, preferred_element_type=F32)


def mm_tn(left, right):
    return lax.dot_general(left, right, (((0,), (0,)), ((), ())), preferred_element_type=F32)


def mm_nt(left, right):
    return lax.dot_general(left, right, (((1,), (1,)), ((), ())), preferred_element_type=F32)


def mm3(left, right):
    left_high, left_low = split(left)
    right_high, right_low = split(right)
    return mm(left_high, right_high) + (mm(left_high, right_low) + mm(left_low, right_high))


def column(row_ref, count):
    diagonal = lax.broadcasted_iota(jnp.int32, (count, count), 0) == lax.broadcasted_iota(
        jnp.int32, (count, count), 1
    )
    return jnp.sum(jnp.where(diagonal, row_ref[...], 0), axis=1, keepdims=True)


def pack_kernel(
    live_ref, resid_hbm, front_hbm, row_hbm, out_ref, resid_ref, front_ref, row_ref, sems
):
    copies = [
        pltpu.make_async_copy(source, target, sems.at[index])
        for index, (source, target) in enumerate(
            ((front_hbm, front_ref), (row_hbm, row_ref), (resid_hbm, resid_ref))
        )
    ]
    for copy in copies:
        copy.start()
    recv = resid_ref.shape[0]
    live = lax.broadcasted_iota(jnp.int32, (recv, 1), 0) < live_ref[0]
    copies[0].wait()
    front = column(front_ref, recv)
    copies[1].wait()
    rows = jnp.where(live, column(row_ref, recv) + 1, 0)
    onehot = front == lax.broadcasted_iota(jnp.int32, (recv, FRONT), 1)
    earlier = lax.broadcasted_iota(jnp.int32, (recv, recv), 0) > lax.broadcasted_iota(
        jnp.int32, (recv, recv), 1
    )
    before = mm(earlier.astype(F32).astype(BF16), onehot.astype(F32).astype(BF16))
    position = jnp.sum(jnp.where(onehot, before, 0.0), axis=1, keepdims=True)
    slot = front * SLOTS + position.astype(jnp.int32)
    place = slot == lax.broadcasted_iota(jnp.int32, (recv, FRONT * SLOTS), 1)
    place = place.astype(F32).astype(BF16)
    copies[2].wait()
    high, mid, low = split3(jnp.where(live, resid_ref[...], 0.0))
    coarse = jnp.broadcast_to((rows & ~15).astype(F32), (recv, 128)).astype(BF16)
    fine = jnp.broadcast_to((rows & 15).astype(F32), (recv, 128)).astype(BF16)
    out_ref[:, :SHOTS] = mm_tn(place, high) + (mm_tn(place, mid) + mm_tn(place, low))
    out_ref[:, SHOTS:] = mm_tn(place, coarse) + mm_tn(place, fine)


def local_kernel(
    rhs_hbm, dinv_hbm, u_hbm, v_hbm,
    own_hbm, up_hbm, down_hbm, mine_ref, send_ref,
    rhs_ref, dinv_ref, u_ref, v_ref, own_ref, up_ref, down_ref, wide_ref, narrow_ref,
    in_sems, out_sems,
):
    core = lax.axis_index("core")
    loads = []
    for level in range(LEVELS):
        pairs = [(dinv_hbm, dinv_ref)]
        if level < LEVELS - 1:
            pairs += [(rhs_hbm, rhs_ref), (u_hbm, u_ref), (v_hbm, v_ref)]
        loads.append(
            [
                pltpu.make_async_copy(source.at[level], target.at[level], in_sems.at[level, index])
                for index, (source, target) in enumerate(pairs)
            ]
        )
        for copy in loads[-1]:
            copy.start()
    stores = []

    def keep(source, target):
        copy = pltpu.make_async_copy(source, target, out_sems.at[len(stores)])
        copy.start()
        stores.append(copy)

    def reduce(factor, pair):
        return mm_tn(factor, pair[0]) + mm_tn(factor, pair[1])

    def save(at, value):
        scratch = narrow_ref if value.shape[1] == 128 else wide_ref
        scratch[...] = value
        for piece in range(value.shape[1] // 128):
            rows = pl.ds(at + piece, HALF, stride=PART)
            lanes = slice(piece * 128, piece * 128 + 128)
            mine_ref[rows, :] = scratch[pl.ds(core * HALF, HALF), lanes]
            send_ref[rows, :] = scratch[pl.ds((1 - core) * HALF, HALF), lanes]

    mine_ref[...] = jnp.zeros_like(mine_ref)
    send_ref[...] = jnp.zeros_like(send_ref)
    for level in range(LEVELS):
        for copy in loads[level]:
            copy.wait()
        block = dinv_ref[level]
        if level > 0:
            down = split(mm(block, v_ref[level - 1]))
            down_ref[level - 1, 0], down_ref[level - 1, 1] = down
            keep(down_ref.at[level - 1], down_hbm.at[level - 1])
        if level == LEVELS - 1:
            continue
        own = mm(block, rhs_ref[level])
        own_ref[level] = own
        keep(own_ref.at[level], own_hbm.at[level])
        up = split(mm(block, u_ref[level]))
        up_ref[level, 0], up_ref[level, 1] = up
        keep(up_ref.at[level], up_hbm.at[level])
        own = split(own)
        save((S0, S1, S2)[level], reduce(u_ref[level], own))
        save((B0, B1, B2)[level], reduce(u_ref[level], up))
        if level > 0:
            save((None, R0V, R1V)[level], reduce(v_ref[level - 1], own))
            save((None, A1, A2)[level], reduce(v_ref[level - 1], up))
            save((None, C1, C2)[level], reduce(u_ref[level], down))
    for copy in stores:
        copy.wait()


def bottom_kernel(got_ref, dinv_ref, v_ref, rhs_ref, forward_ref, coupled_ref):
    rowid = got_ref[:, SHOTS:]
    lane = lax.broadcasted_iota(jnp.int32, rowid.shape, 1).astype(F32) + 1.0
    select = jnp.concatenate(
        [(rowid == lane + 128.0 * part).astype(F32).astype(BF16) for part in range(ROWS // 128)],
        axis=1,
    )
    high, mid, low = split3(got_ref[:, :SHOTS])
    block = dinv_ref[LEVELS - 1]
    chosen = mm_nt(block, select).astype(BF16)
    forward = mm(block, rhs_ref[LEVELS - 1]) + (mm(chosen, high) + (mm(chosen, mid) + mm(chosen, low)))
    forward_ref[...] = forward
    high, low = split(forward)
    factor = v_ref[LEVELS - 2]
    coupled_ref[...] = mm_tn(factor, high) + mm_tn(factor, low)


def message_kernel(coupled_ref, mine_ref, other_ref, out_ref):
    for front in range(FRONT):
        early = slice(front * EARLY, front * EARLY + EARLY)
        base = front * MESSAGE
        out_ref[base : base + EARLY, :] = mine_ref[early, :] + other_ref[early, :]
        for half in range(2):
            rows = slice(half * HALF + 4 * front, half * HALF + 4 * front + 4)
            for piece in range(2):
                at = base + EARLY + half * 8 + piece * 4
                out_ref[at : at + 4, :] = coupled_ref[rows, piece * 128 : piece * 128 + 128]


def total_kernel(pieces_ref, out_ref):
    core = lax.axis_index("core")
    total = pieces_ref[0]
    for index in range(1, FRONT):
        total = total + pieces_ref[index]
    out_ref[...] = jnp.zeros_like(out_ref)
    for zl in range(4):
        out_ref[zl * 2 + core, :S2] = total[zl * PART : zl * PART + S2]
        for other in range(4):
            at = CROSS + NODE * other
            out_ref[zl * 2 + core, at : at + NODE] = total[
                other * PART + S2 : other * PART + S2 + NODE
            ]
        for half in range(2):
            for piece in range(2):
                at = EARLY + half * 8 + piece * 4 + zl
                out_ref[zl * 2 + half, R2V + piece : R2V + piece + 1] = total[at : at + 1]


def share_kernel(pieces_ref, cross_ref, node_ref):
    total = pieces_ref[0]
    for index in range(1, 8):
        total = total + pieces_ref[index]
    for index in range(16):
        cross_ref[index] = total[:CROSS]
    node_ref[...] = total[CROSS:]


def nodes_kernel(cross_ref, node_ref, out_ref):
    zh = lax.axis_index("zh")
    order = [zh, zh ^ 1, zh ^ 2, zh ^ 3]
    for zl in range(4):
        nodes = [cross_ref[node * 4 + zl] for node in order]
        pair, other = nodes[0] + nodes[1], nodes[2] + nodes[3]
        total = pair + other
        spread = jnp.concatenate(
            [node[R2V : R2V + 2] for node in nodes]
            + [node[A2 : A2 + 1] for node in nodes]
            + [value[R1V : R1V + 2] for value in (pair, other)]
            + [value[A1 : A1 + 1] for value in (pair, other)]
            + [total[R0V : R0V + 5], pair[S1 : S1 + 4]]
            + [node_ref[NODE * zl : NODE * zl + NODE], jnp.zeros((1, 128), F32)],
            axis=0,
        )
        for front in range(FRONT):
            out_ref[front, zl * SPREAD : zl * SPREAD + SPREAD] = spread


def solve_kernel(
    rank_ref, mine_ref, other_ref, own_ref, forward_ref, up_ref, down_ref, out_hbm,
    out_ref, out_sems,
):
    stores = []

    def finish(level, value):
        out_ref[level] = value
        copy = pltpu.make_async_copy(out_ref.at[level], out_hbm.at[level], out_sems.at[level])
        copy.start()
        stores.append(copy)

    first = lax.axis_index("core") == 0

    def block(at):
        mine = mine_ref[pl.ds(at, HALF, stride=SPREAD), :]
        other = other_ref[pl.ds(at, HALF, stride=SPREAD), :]
        return jnp.concatenate(
            [jnp.where(first, mine, other), jnp.where(first, other, mine)], axis=0
        )

    def wide(at):
        return jnp.concatenate([block(at), block(at + 1)], axis=1)

    def mask(coupling, value):
        keep = lax.broadcasted_iota(jnp.int32, value.shape, 0) < rank_ref[:, coupling : coupling + 1]
        return jnp.where(keep, value, 0.0)

    def expand(pair_ref, index, value):
        high, low = split(value)
        left_high, left_low = pair_ref[index, 0], pair_ref[index, 1]
        return mm(left_high, high) + (mm(left_high, low) + mm(left_low, high))

    c2 = [mask(2, wide(G_R2V + 2 * node)) for node in range(4)]
    t1 = [mm3(block(G_A2 + node), c2[node]) for node in range(4)]
    c1 = [mask(1, wide(G_R1V + 2 * half) - (t1[2 * half] + t1[2 * half + 1])) for half in range(2)]
    t0 = [mm3(block(G_A1 + half), c1[half]) for half in range(2)]
    c0 = mask(0, wide(G_R0V) - (t0[0] + t0[1]))
    d0 = mask(0, wide(G_S0) - mm3(block(G_B0), c0))
    d1 = mask(1, wide(G_S1) - mm3(block(G_B1), c1[0]) - mm3(block(G_C1), d0))
    d2 = mask(2, wide(G_S2) - mm3(block(G_B2), c2[0]) - mm3(block(G_C2), d1))
    finish(0, own_ref[0] - expand(up_ref, 0, c0))
    finish(1, own_ref[1] - expand(up_ref, 1, c1[0]) - expand(down_ref, 0, d0))
    finish(2, own_ref[2] - expand(up_ref, 2, c2[0]) - expand(down_ref, 1, d1))
    finish(3, forward_ref[...] - expand(down_ref, 2, d2))
    for copy in stores:
        copy.wait()


def per_device(rhs, dinv, u_factor, v_factor, rank_sizes, resid, dest_front, dest_row, live_count):

    front = ("x", "y")
    swap = [(0, 1), (1, 0)]

    packed = pl.pallas_call(
        pack_kernel,
        out_shape=jax.ShapeDtypeStruct((FRONT * SLOTS, SHOTS + 128), F32),
        in_specs=[SMEM, HBM, HBM, HBM],
        out_specs=VMEM,
        scratch_shapes=[
            pltpu.VMEM(resid.shape, F32),
            pltpu.VMEM((1, resid.shape[0]), jnp.int32),
            pltpu.VMEM((1, resid.shape[0]), jnp.int32),
            pltpu.SemaphoreType.DMA((3,)),
        ],
        compiler_params=params(WHOLE),
    )(live_count, resid, dest_front.reshape(1, -1), dest_row.reshape(1, -1))
    packed, dinv_after = lax.optimization_barrier((packed, dinv))
    got = lax.all_to_all(
        packed.reshape(FRONT, SLOTS, SHOTS + 128), front, 0, 0, tiled=True
    ).reshape(FRONT * SLOTS, SHOTS + 128)

    pair = jax.ShapeDtypeStruct((LEVELS - 1, 2, ROWS, RANK), BF16)
    early = jax.ShapeDtypeStruct((HALF * PART, 128), F32)
    own, up, down, mine, send = pl.pallas_call(
        local_kernel,
        out_shape=(
            jax.ShapeDtypeStruct((LEVELS - 1, ROWS, SHOTS), F32),
            pair,
            pair,
            early,
            early,
        ),
        in_specs=[HBM] * 4,
        out_specs=(HBM,) * 3 + (VMEM,) * 2,
        scratch_shapes=[
            pltpu.VMEM(rhs.shape, BF16),
            pltpu.VMEM(dinv.shape, BF16),
            pltpu.VMEM(u_factor.shape, BF16),
            pltpu.VMEM(v_factor.shape, BF16),
            pltpu.VMEM((LEVELS - 1, ROWS, SHOTS), F32),
            pltpu.VMEM(pair.shape, BF16),
            pltpu.VMEM(pair.shape, BF16),
            pltpu.VMEM((RANK, SHOTS), F32),
            pltpu.VMEM((RANK, RANK), F32),
            pltpu.SemaphoreType.DMA((LEVELS, 4)),
            pltpu.SemaphoreType.DMA((9,)),
        ],
        compiler_params=params(WHOLE),
        cost_estimate=pl.CostEstimate(
            flops=2_000_000_000, bytes_accessed=8_000_000, transcendentals=0
        ),
    )(rhs, dinv_after, u_factor, v_factor)
    got, send = lax.optimization_barrier((got, send))
    other = lax.ppermute(send, "core", swap)

    forward, coupled = pl.pallas_call(
        bottom_kernel,
        out_shape=(
            jax.ShapeDtypeStruct((ROWS, SHOTS), F32),
            jax.ShapeDtypeStruct((RANK, SHOTS), F32),
        ),
        in_specs=[VMEM] * 4,
        out_specs=(VMEM, VMEM),
        compiler_params=params(8),
    )(got, dinv, v_factor, rhs)
    message = pl.pallas_call(
        message_kernel,
        out_shape=jax.ShapeDtypeStruct((FRONT * MESSAGE, 128), F32),
        in_specs=[VMEM] * 3,
        out_specs=VMEM,
        compiler_params=params(4),
    )(coupled, mine, other)
    pieces = lax.all_to_all(message.reshape(FRONT, MESSAGE, 128), front, 0, 0, tiled=True)
    summed = pl.pallas_call(
        total_kernel,
        out_shape=jax.ShapeDtypeStruct((8, SENT, 128), F32),
        in_specs=[VMEM],
        out_specs=VMEM,
        compiler_params=params(4),
    )(pieces)
    pieces = lax.all_to_all(summed, ("zl", "core"), 0, 0, tiled=True)
    cross, node = pl.pallas_call(
        share_kernel,
        out_shape=(
            jax.ShapeDtypeStruct((16, CROSS, 128), F32),
            jax.ShapeDtypeStruct((4 * NODE, 128), F32),
        ),
        in_specs=[VMEM],
        out_specs=(VMEM, VMEM),
        compiler_params=params(4),
    )(pieces)
    cross = lax.all_to_all(cross, ("zh", "zl"), 0, 0, tiled=True)
    spread = pl.pallas_call(
        nodes_kernel,
        out_shape=jax.ShapeDtypeStruct((FRONT, 4 * SPREAD, 128), F32),
        in_specs=[VMEM, VMEM],
        out_specs=VMEM,
        compiler_params=params(4),
    )(cross, node)
    gathered = lax.all_to_all(spread, front, 0, 0, tiled=True).reshape(HALF * SPREAD, 128)
    other = lax.ppermute(gathered, "core", swap)

    return pl.pallas_call(
        solve_kernel,
        out_shape=jax.ShapeDtypeStruct((LEVELS, ROWS, SHOTS), F32),
        in_specs=[VMEM] * 7,
        out_specs=HBM,
        scratch_shapes=[
            pltpu.VMEM((LEVELS, ROWS, SHOTS), F32),
            pltpu.SemaphoreType.DMA((LEVELS,)),
        ],
        compiler_params=params(SOLVE),
    )(rank_sizes.reshape(1, -1), gathered, other, own, forward, up, down)


def solution(mesh):
    grid = Mesh(mesh.devices.reshape(4, 4, 2, 4, 4), ALL)
    wide = P(None, ALL, None)
    return jax.shard_map(
        per_device,
        mesh=grid,
        in_specs=(wide, wide, wide, wide, P(), P(ALL, None), P(ALL, None), P(ALL), P(ALL)),
        out_specs=wide,
        check_vma=False,
    )
```

```python
import functools

import jax
import jax.numpy as jnp
from jax import lax
from jax.experimental import pallas as pl
from jax.experimental.pallas import tpu as pltpu
from jax.sharding import Mesh
from jax.sharding import PartitionSpec as P

F32 = jnp.float32
BF16 = jnp.bfloat16
LEVELS = 4
RANK = 128
SHOTS = 256
ROWS = 384
SLOTS = 8
FRONT = 16
HALF = RANK // 2
PART = 18
EARLY = 4 * PART
MESSAGE = EARLY + 16
SENT = 32
CROSS = 16
NODE = 4
SPREAD = 32
ALL = ("zh", "zl", "core", "x", "y")

A2, R1V, A1, R0V, S0, B0, S1, B1, C1, S2, B2, C2 = 0, 1, 3, 4, 6, 8, 9, 11, 12, 13, 15, 16
R2V = S2
G_R2V, G_A2, G_R1V, G_A1, G_R0V, G_S0, G_B0, G_S1, G_B1, G_C1, G_S2, G_B2, G_C2 = (
    0, 8, 12, 16, 18, 20, 22, 23, 25, 26, 27, 29, 30,
)


SOLVE = 16
LOCAL = 54
WHOLE = 54


def params(mebibytes):
    return pltpu.CompilerParams(vmem_limit_bytes=int(mebibytes * 2**20))


VMEM = pl.BlockSpec(memory_space=pltpu.VMEM)
SMEM = pl.BlockSpec(memory_space=pltpu.SMEM)
HBM = pl.BlockSpec(memory_space=pltpu.HBM)


def split(value):
    high = value.astype(BF16)
    return high, (value - high.astype(F32)).astype(BF16)


def split3(value):
    high = value.astype(BF16)
    rest = value - high.astype(F32)
    mid = rest.astype(BF16)
    return high, mid, (rest - mid.astype(F32)).astype(BF16)


def mm(left, right):
    return jnp.dot(left, right, preferred_element_type=F32)


def mm_tn(left, right):
    return lax.dot_general(left, right, (((0,), (0,)), ((), ())), preferred_element_type=F32)


def mm_nt(left, right):
    return lax.dot_general(left, right, (((1,), (1,)), ((), ())), preferred_element_type=F32)


def mm3(left, right):
    left_high, left_low = split(left)
    right_high, right_low = split(right)
    return mm(left_high, right_high) + (mm(left_high, right_low) + mm(left_low, right_high))


def column(row_ref, count):
    diagonal = lax.broadcasted_iota(jnp.int32, (count, count), 0) == lax.broadcasted_iota(
        jnp.int32, (count, count), 1
    )
    return jnp.sum(jnp.where(diagonal, row_ref[...], 0), axis=1, keepdims=True)


def pack_kernel(
    live_ref, resid_hbm, front_hbm, row_hbm, out_ref, resid_ref, front_ref, row_ref, sems
):
    copies = [
        pltpu.make_async_copy(source, target, sems.at[index])
        for index, (source, target) in enumerate(
            ((front_hbm, front_ref), (row_hbm, row_ref), (resid_hbm, resid_ref))
        )
    ]
    for copy in copies:
        copy.start()
    recv = resid_ref.shape[0]
    live = lax.broadcasted_iota(jnp.int32, (recv, 1), 0) < live_ref[0]
    copies[0].wait()
    front = column(front_ref, recv)
    copies[1].wait()
    rows = jnp.where(live, column(row_ref, recv) + 1, 0)
    same = (front == front_ref[...]) & (
        lax.broadcasted_iota(jnp.int32, (recv, recv), 1)
        < lax.broadcasted_iota(jnp.int32, (recv, recv), 0)
    )
    position = jnp.sum(same.astype(jnp.int32), axis=1, keepdims=True)
    slot = front * SLOTS + position
    place = slot == lax.broadcasted_iota(jnp.int32, (recv, FRONT * SLOTS), 1)
    place = place.astype(F32).astype(BF16)
    copies[2].wait()
    high, mid, low = split3(jnp.where(live, resid_ref[...], 0.0))
    coarse = jnp.broadcast_to((rows & ~15).astype(F32), (recv, 128)).astype(BF16)
    fine = jnp.broadcast_to((rows & 15).astype(F32), (recv, 128)).astype(BF16)
    out_ref[:, :SHOTS] = mm_tn(place, high) + (mm_tn(place, mid) + mm_tn(place, low))
    out_ref[:, SHOTS:] = mm_tn(place, coarse) + mm_tn(place, fine)


def local_kernel(
    rhs_hbm, dinv_hbm, u_hbm, v_hbm, mine_ref, send_ref,
    rhs_ref, dinv_ref, u_ref, v_ref, wide_ref, narrow_ref, sems,
):
    core = lax.axis_index("core")
    loads = []
    for level in range(LEVELS - 1):
        pairs = [
            (dinv_hbm.at[level], dinv_ref.at[level]),
            (rhs_hbm.at[level], rhs_ref.at[level]),
            (u_hbm.at[level], u_ref.at[level]),
        ]
        if level > 0:
            pairs.append((v_hbm.at[level - 1], v_ref.at[level - 1]))
        loads.append(
            [
                pltpu.make_async_copy(source, target, sems.at[level, index])
                for index, (source, target) in enumerate(pairs)
            ]
        )
        for copy in loads[-1]:
            copy.start()

    def reduce(factor, pair):
        return mm_tn(factor, pair[0]) + mm_tn(factor, pair[1])

    def save(at, value):
        scratch = narrow_ref if value.shape[1] == 128 else wide_ref
        scratch[...] = value
        for piece in range(value.shape[1] // 128):
            rows = pl.ds(at + piece, HALF, stride=PART)
            lanes = slice(piece * 128, piece * 128 + 128)
            mine_ref[rows, :] = scratch[pl.ds(core * HALF, HALF), lanes]
            send_ref[rows, :] = scratch[pl.ds((1 - core) * HALF, HALF), lanes]

    save(PART - 1, jnp.zeros((RANK, 128), F32))
    for level in range(LEVELS - 1):
        for copy in loads[level]:
            copy.wait()
        block = dinv_ref[level]
        own = split(mm(block, rhs_ref[level]))
        up = split(mm(block, u_ref[level]))
        save((S0, S1, S2)[level], reduce(u_ref[level], own))
        save((B0, B1, B2)[level], reduce(u_ref[level], up))
        if level > 0:
            down = split(mm(block, v_ref[level - 1]))
            save((None, R0V, R1V)[level], reduce(v_ref[level - 1], own))
            save((None, A1, A2)[level], reduce(v_ref[level - 1], up))
            save((None, C1, C2)[level], reduce(u_ref[level], down))


def fields_kernel(rhs_ref, dinv_ref, u_ref, v_ref, own_ref, mix_ref):
    for level in range(LEVELS):
        block = dinv_ref[level]
        if level < LEVELS - 1:
            own_ref[level] = mm(block, rhs_ref[level])
            for part, value in enumerate(split(mm(block, u_ref[level]))):
                mix_ref[level, part, :, :RANK] = value
        if level > 0:
            for part, value in enumerate(split(mm(block, v_ref[level - 1]))):
                mix_ref[level, part, :, RANK:] = value


def bottom_kernel(got_ref, dinv_ref, v_ref, rhs_ref, forward_ref, coupled_ref):
    rowid = got_ref[:, SHOTS:]
    lane = lax.broadcasted_iota(jnp.int32, rowid.shape, 1).astype(F32) + 1.0
    select = jnp.concatenate(
        [(rowid == lane + 128.0 * part).astype(F32).astype(BF16) for part in range(ROWS // 128)],
        axis=1,
    )
    high, mid, low = split3(got_ref[:, :SHOTS])
    block = dinv_ref[LEVELS - 1]
    chosen = mm_nt(block, select).astype(BF16)
    forward = mm(block, rhs_ref[LEVELS - 1]) + (mm(chosen, high) + (mm(chosen, mid) + mm(chosen, low)))
    forward_ref[...] = forward
    high, low = split(forward)
    factor = v_ref[LEVELS - 2]
    coupled_ref[...] = mm_tn(factor, high) + mm_tn(factor, low)


def message_kernel(coupled_ref, mine_ref, other_ref, out_ref):
    for front in range(FRONT):
        early = slice(front * EARLY, front * EARLY + EARLY)
        base = front * MESSAGE
        out_ref[base : base + EARLY, :] = mine_ref[early, :] + other_ref[early, :]
        for half in range(2):
            rows = slice(half * HALF + 4 * front, half * HALF + 4 * front + 4)
            for piece in range(2):
                at = base + EARLY + half * 8 + piece * 4
                out_ref[at : at + 4, :] = coupled_ref[rows, piece * 128 : piece * 128 + 128]


def total_kernel(pieces_ref, out_ref):
    core = lax.axis_index("core")
    total = pieces_ref[0]
    for index in range(1, FRONT):
        total = total + pieces_ref[index]
    out_ref[...] = jnp.zeros_like(out_ref)
    for zl in range(4):
        out_ref[zl * 2 + core, :S2] = total[zl * PART : zl * PART + S2]
        for other in range(4):
            at = CROSS + NODE * other
            out_ref[zl * 2 + core, at : at + NODE] = total[
                other * PART + S2 : other * PART + S2 + NODE
            ]
        for half in range(2):
            for piece in range(2):
                at = EARLY + half * 8 + piece * 4 + zl
                out_ref[zl * 2 + half, R2V + piece : R2V + piece + 1] = total[at : at + 1]


def share_kernel(pieces_ref, cross_ref, node_ref):
    total = pieces_ref[0]
    for index in range(1, 8):
        total = total + pieces_ref[index]
    for index in range(16):
        cross_ref[index] = total[:CROSS]
    node_ref[...] = total[CROSS:]


def nodes_kernel(cross_ref, node_ref, out_ref):
    zh = lax.axis_index("zh")
    order = [zh, zh ^ 1, zh ^ 2, zh ^ 3]
    for zl in range(4):
        nodes = [cross_ref[node * 4 + zl] for node in order]
        pair, other = nodes[0] + nodes[1], nodes[2] + nodes[3]
        total = pair + other
        spread = jnp.concatenate(
            [node[R2V : R2V + 2] for node in nodes]
            + [node[A2 : A2 + 1] for node in nodes]
            + [value[R1V : R1V + 2] for value in (pair, other)]
            + [value[A1 : A1 + 1] for value in (pair, other)]
            + [total[R0V : R0V + 5], pair[S1 : S1 + 4]]
            + [node_ref[NODE * zl : NODE * zl + NODE], jnp.zeros((1, 128), F32)],
            axis=0,
        )
        for front in range(FRONT):
            out_ref[front, zl * SPREAD : zl * SPREAD + SPREAD] = spread


def solve_kernel(
    rank_ref, mine_ref, other_ref, own_ref, forward_ref, mix_ref, out_hbm,
    out_ref, out_sems,
):
    def solve(low_ref, high_ref):
        stores = []

        def finish(level, value):
            out_ref[level] = value
            copy = pltpu.make_async_copy(out_ref.at[level], out_hbm.at[level], out_sems.at[level])
            copy.start()
            stores.append(copy)

        def block(at):
            rows = pl.ds(at, HALF, stride=SPREAD)
            return jnp.concatenate([low_ref[rows, :], high_ref[rows, :]], axis=0)

        def wide(at):
            return jnp.concatenate([block(at), block(at + 1)], axis=1)

        def mask(coupling, value):
            keep = lax.broadcasted_iota(jnp.int32, value.shape, 0) < rank_ref[:, coupling : coupling + 1]
            return jnp.where(keep, value, 0.0)

        def expand(level, lanes, *values):
            high, low = split(jnp.concatenate(values, axis=0))
            left_high, left_low = mix_ref[level, 0, :, lanes], mix_ref[level, 1, :, lanes]
            return mm(left_high, high) + (mm(left_high, low) + mm(left_low, high))

        def couple(blocks, values):
            left = [block(at) for at in blocks]
            return mm3(jnp.concatenate(left, axis=1), jnp.concatenate(values, axis=0))

        c2 = [mask(2, wide(G_R2V + 2 * node)) for node in range(4)]
        t1 = [
            couple((G_A2 + 2 * half, G_A2 + 2 * half + 1), c2[2 * half : 2 * half + 2])
            for half in range(2)
        ]
        c1 = [mask(1, wide(G_R1V + 2 * half) - t1[half]) for half in range(2)]
        c0 = mask(0, wide(G_R0V) - couple((G_A1, G_A1 + 1), c1))
        d0 = mask(0, wide(G_S0) - couple((G_B0,), (c0,)))
        finish(0, own_ref[0] - expand(0, slice(0, RANK), c0))
        d1 = mask(1, wide(G_S1) - couple((G_B1, G_C1), (c1[0], d0)))
        finish(1, own_ref[1] - expand(1, slice(0, 2 * RANK), c1[0], d0))
        d2 = mask(2, wide(G_S2) - couple((G_B2, G_C2), (c2[0], d1)))
        finish(2, own_ref[2] - expand(2, slice(0, 2 * RANK), c2[0], d1))
        finish(3, forward_ref[...] - expand(3, slice(RANK, 2 * RANK), d2))
        for copy in stores:
            copy.wait()

    core = lax.axis_index("core")
    pl.when(core == 0)(lambda: solve(mine_ref, other_ref))
    pl.when(core == 1)(lambda: solve(other_ref, mine_ref))


def per_device(rhs, dinv, u_factor, v_factor, rank_sizes, resid, dest_front, dest_row, live_count):

    front = ("x", "y")
    swap = [(0, 1), (1, 0)]

    packed = pl.pallas_call(
        pack_kernel,
        out_shape=jax.ShapeDtypeStruct((FRONT * SLOTS, SHOTS + 128), F32),
        in_specs=[SMEM, HBM, HBM, HBM],
        out_specs=VMEM,
        scratch_shapes=[
            pltpu.VMEM(resid.shape, F32),
            pltpu.VMEM((1, resid.shape[0]), jnp.int32),
            pltpu.VMEM((1, resid.shape[0]), jnp.int32),
            pltpu.SemaphoreType.DMA((3,)),
        ],
        compiler_params=params(WHOLE),
    )(live_count, resid, dest_front.reshape(1, -1), dest_row.reshape(1, -1))
    packed, dinv_after = lax.optimization_barrier((packed, dinv))
    got = lax.all_to_all(
        packed.reshape(FRONT, SLOTS, SHOTS + 128), front, 0, 0, tiled=True
    ).reshape(FRONT * SLOTS, SHOTS + 128)

    early = jax.ShapeDtypeStruct((HALF * PART, 128), F32)
    mine, send = pl.pallas_call(
        local_kernel,
        out_shape=(early, early),
        in_specs=[HBM] * 4,
        out_specs=(VMEM, VMEM),
        scratch_shapes=[
            pltpu.VMEM((LEVELS - 1, ROWS, SHOTS), BF16),
            pltpu.VMEM((LEVELS - 1, ROWS, ROWS), BF16),
            pltpu.VMEM((LEVELS - 1, ROWS, RANK), BF16),
            pltpu.VMEM((LEVELS - 2, ROWS, RANK), BF16),
            pltpu.VMEM((RANK, SHOTS), F32),
            pltpu.VMEM((RANK, RANK), F32),
            pltpu.SemaphoreType.DMA((LEVELS - 1, 4)),
        ],
        compiler_params=params(LOCAL),
        cost_estimate=pl.CostEstimate(
            flops=20_000_000_000, bytes_accessed=8_000_000, transcendentals=0
        ),
    )(rhs, dinv_after, u_factor, v_factor)
    other = lax.ppermute(send, "core", swap)

    forward, coupled = pl.pallas_call(
        bottom_kernel,
        out_shape=(
            jax.ShapeDtypeStruct((ROWS, SHOTS), F32),
            jax.ShapeDtypeStruct((RANK, SHOTS), F32),
        ),
        in_specs=[VMEM] * 4,
        out_specs=(VMEM, VMEM),
        compiler_params=params(8),
        cost_estimate=pl.CostEstimate(
            flops=20_000_000_000, bytes_accessed=4_000_000, transcendentals=0
        ),
    )(got, dinv, v_factor, rhs)
    message = pl.pallas_call(
        message_kernel,
        out_shape=jax.ShapeDtypeStruct((FRONT * MESSAGE, 128), F32),
        in_specs=[VMEM] * 3,
        out_specs=VMEM,
        compiler_params=params(4),
    )(coupled, mine, other)

    message, dinv_late = lax.optimization_barrier((message, dinv))
    own, mix = pl.pallas_call(
        fields_kernel,
        out_shape=(
            jax.ShapeDtypeStruct((LEVELS - 1, ROWS, SHOTS), F32),
            jax.ShapeDtypeStruct((LEVELS, 2, ROWS, 2 * RANK), BF16),
        ),
        in_specs=[VMEM] * 4,
        out_specs=(VMEM,) * 2,
        compiler_params=params(8),
        cost_estimate=pl.CostEstimate(
            flops=1_200_000_000, bytes_accessed=5_000_000, transcendentals=0
        ),
    )(rhs, dinv_late, u_factor, v_factor)
    pieces = lax.all_to_all(message.reshape(FRONT, MESSAGE, 128), front, 0, 0, tiled=True)
    summed = pl.pallas_call(
        total_kernel,
        out_shape=jax.ShapeDtypeStruct((8, SENT, 128), F32),
        in_specs=[VMEM],
        out_specs=VMEM,
        compiler_params=params(4),
    )(pieces)
    pieces = lax.all_to_all(summed, ("zl", "core"), 0, 0, tiled=True)
    cross, node = pl.pallas_call(
        share_kernel,
        out_shape=(
            jax.ShapeDtypeStruct((16, CROSS, 128), F32),
            jax.ShapeDtypeStruct((4 * NODE, 128), F32),
        ),
        in_specs=[VMEM],
        out_specs=(VMEM, VMEM),
        compiler_params=params(4),
    )(pieces)
    cross = lax.all_to_all(cross, ("zh", "zl"), 0, 0, tiled=True)
    spread = pl.pallas_call(
        nodes_kernel,
        out_shape=jax.ShapeDtypeStruct((FRONT, 4 * SPREAD, 128), F32),
        in_specs=[VMEM, VMEM],
        out_specs=VMEM,
        compiler_params=params(4),
    )(cross, node)
    gathered = lax.all_to_all(spread, front, 0, 0, tiled=True).reshape(HALF * SPREAD, 128)
    other = lax.ppermute(gathered, "core", swap)

    return pl.pallas_call(
        solve_kernel,
        out_shape=jax.ShapeDtypeStruct((LEVELS, ROWS, SHOTS), F32),
        in_specs=[VMEM] * 6,
        out_specs=HBM,
        scratch_shapes=[
            pltpu.VMEM((LEVELS, ROWS, SHOTS), F32),
            pltpu.SemaphoreType.DMA((LEVELS,)),
        ],
        compiler_params=params(SOLVE),
    )(rank_sizes.reshape(1, -1), gathered, other, own, forward, mix)


def solution(mesh):
    grid = Mesh(mesh.devices.reshape(4, 4, 2, 4, 4), ALL)
    wide = P(None, ALL, None)
    return jax.shard_map(
        per_device,
        mesh=grid,
        in_specs=(wide, wide, wide, wide, P(), P(ALL, None), P(ALL, None), P(ALL), P(ALL)),
        out_specs=wide,
        check_vma=False,
    )
```

```python
import functools

import jax
import jax.numpy as jnp
from jax import lax
from jax.experimental import pallas as pl
from jax.experimental.pallas import tpu as pltpu
from jax.sharding import Mesh
from jax.sharding import PartitionSpec as P

F32 = jnp.float32
BF16 = jnp.bfloat16
LEVELS = 4
RANK = 128
SHOTS = 256
ROWS = 384
SLOTS = 8
FRONT = 16
HALF = RANK // 2
PART = 18
EARLY = 4 * PART
MESSAGE = EARLY + 16
SENT = 32
CROSS = 16
NODE = 4
SPREAD = 32
ALL = ("zh", "zl", "core", "x", "y")

A2, R1V, A1, R0V, S0, B0, S1, B1, C1, S2, B2, C2 = 0, 1, 3, 4, 6, 8, 9, 11, 12, 13, 15, 16
R2V = S2
G_R2V, G_A2, G_R1V, G_A1, G_R0V, G_S0, G_B0, G_S1, G_B1, G_C1, G_S2, G_B2, G_C2 = (
    0, 8, 12, 16, 18, 20, 22, 23, 25, 26, 27, 29, 30,
)


SOLVE = 16
LOCAL = 54
WHOLE = 54


def params(mebibytes):
    return pltpu.CompilerParams(vmem_limit_bytes=int(mebibytes * 2**20))


VMEM = pl.BlockSpec(memory_space=pltpu.VMEM)
HBM = pl.BlockSpec(memory_space=pltpu.HBM)


def split(value):
    high = value.astype(BF16)
    return high, (value - high.astype(F32)).astype(BF16)


def split3(value):
    high = value.astype(BF16)
    rest = value - high.astype(F32)
    mid = rest.astype(BF16)
    return high, mid, (rest - mid.astype(F32)).astype(BF16)


def mm(left, right):
    return jnp.dot(left, right, preferred_element_type=F32)


def mm_tn(left, right):
    return lax.dot_general(left, right, (((0,), (0,)), ((), ())), preferred_element_type=F32)


def mm_nt(left, right):
    return lax.dot_general(left, right, (((1,), (1,)), ((), ())), preferred_element_type=F32)


def mm3(left, right):
    left_high, left_low = split(left)
    right_high, right_low = split(right)
    return mm(left_high, right_high) + (mm(left_high, right_low) + mm(left_low, right_high))


def pack_kernel(
    live_hbm, resid_hbm, front_hbm, row_hbm, out_ref,
    live_ref, resid_ref, front_ref, row_ref, sems,
):
    copies = [
        pltpu.make_async_copy(source, target, sems.at[index])
        for index, (source, target) in enumerate(
            (
                (front_hbm, front_ref),
                (row_hbm, row_ref),
                (resid_hbm, resid_ref),
                (live_hbm, live_ref),
            )
        )
    ]
    for copy in copies:
        copy.start()
    recv = resid_ref.shape[0]
    sublane = lax.broadcasted_iota(jnp.int32, (recv, recv), 0)
    lane = lax.broadcasted_iota(jnp.int32, (recv, recv), 1)
    copies[0].wait()
    front = front_ref[...]
    column = jnp.sum(jnp.where(sublane == lane, front, 0), axis=1, keepdims=True)
    earlier = (column == front) & (sublane < lane)
    slot = front * SLOTS + jnp.sum(earlier.astype(jnp.int32), axis=0, keepdims=True)
    copies[3].wait()
    live = lane[:1] < live_ref[...]
    place = live & (
        lax.broadcasted_iota(jnp.int32, (FRONT * SLOTS, recv), 0) == slot
    )
    copies[1].wait()
    rows = jnp.sum(jnp.where(place, row_ref[...] + 1, 0), axis=1, keepdims=True)
    out_ref[:, SHOTS:] = jnp.broadcast_to(rows.astype(F32), (FRONT * SLOTS, 128))
    place = place.astype(F32).astype(BF16)
    copies[2].wait()
    high, mid, low = split3(resid_ref[...])
    out_ref[:, :SHOTS] = mm(place, high) + (mm(place, mid) + mm(place, low))


def local_kernel(
    rhs_hbm, dinv_hbm, u_hbm, v_hbm, mine_ref, send_ref,
    rhs_ref, dinv_ref, u_ref, v_ref, wide_ref, narrow_ref, sems,
):
    core = lax.axis_index("core")
    loads = []
    for level in range(LEVELS - 1):
        pairs = [
            (dinv_hbm.at[level], dinv_ref.at[level]),
            (rhs_hbm.at[level], rhs_ref.at[level]),
            (u_hbm.at[level], u_ref.at[level]),
        ]
        if level > 0:
            pairs.append((v_hbm.at[level - 1], v_ref.at[level - 1]))
        loads.append(
            [
                pltpu.make_async_copy(source, target, sems.at[level, index])
                for index, (source, target) in enumerate(pairs)
            ]
        )
        for copy in loads[-1]:
            copy.start()

    def save(at, value):
        scratch = narrow_ref if value.shape[1] == 128 else wide_ref
        scratch[...] = value
        for piece in range(value.shape[1] // 128):
            rows = pl.ds(at + piece, HALF, stride=PART)
            lanes = slice(piece * 128, piece * 128 + 128)
            mine_ref[rows, :] = scratch[pl.ds(core * HALF, HALF), lanes]
            send_ref[rows, :] = scratch[pl.ds((1 - core) * HALF, HALF), lanes]

    save(PART - 1, jnp.zeros((RANK, 128), F32))
    for level in range(LEVELS - 1):
        for copy in loads[level]:
            copy.wait()
        block = dinv_ref[level]
        factor = u_ref[level]
        narrow = factor
        if level > 0:
            narrow = jnp.concatenate([factor, v_ref[level - 1]], axis=1)
            factor = narrow
        own = split(mm(block, rhs_ref[level]))
        mix = split(mm(block, narrow))
        own = mm_tn(factor, own[0]) + mm_tn(factor, own[1])
        mix = mm_tn(factor, mix[0]) + mm_tn(factor, mix[1])
        save((S0, S1, S2)[level], own[:RANK])
        save((B0, B1, B2)[level], mix[:RANK, :RANK])
        if level > 0:
            save((None, C1, C2)[level], mix[:RANK, RANK:])
            save((None, R0V, R1V)[level], own[RANK:])
            save((None, A1, A2)[level], mix[RANK:, :RANK])


def fields_kernel(rhs_ref, dinv_ref, u_ref, v_ref, own_ref, mix_ref):
    for level in range(LEVELS):
        block = dinv_ref[level]
        if level < LEVELS - 1:
            own_ref[level] = mm(block, rhs_ref[level])
            for part, value in enumerate(split(mm(block, u_ref[level]))):
                mix_ref[level, part, :, :RANK] = value
        if level > 0:
            for part, value in enumerate(split(mm(block, v_ref[level - 1]))):
                mix_ref[level, part, :, RANK:] = value


def bottom_kernel(got_ref, dinv_ref, v_ref, rhs_ref, forward_ref, coupled_ref):
    rowid = got_ref[:, SHOTS:]
    lane = lax.broadcasted_iota(jnp.int32, rowid.shape, 1).astype(F32) + 1.0
    select = jnp.concatenate(
        [(rowid == lane + 128.0 * part).astype(F32).astype(BF16) for part in range(ROWS // 128)],
        axis=1,
    )
    high, mid, low = split3(got_ref[:, :SHOTS])
    block = dinv_ref[LEVELS - 1]
    chosen = mm_nt(block, select).astype(BF16)
    forward = mm(block, rhs_ref[LEVELS - 1]) + (mm(chosen, high) + (mm(chosen, mid) + mm(chosen, low)))
    forward_ref[...] = forward
    high, low = split(forward)
    factor = v_ref[LEVELS - 2]
    coupled_ref[...] = mm_tn(factor, high) + mm_tn(factor, low)


def message_kernel(coupled_ref, mine_ref, other_ref, out_ref):
    for front in range(FRONT):
        early = slice(front * EARLY, front * EARLY + EARLY)
        base = front * MESSAGE
        out_ref[base : base + EARLY, :] = mine_ref[early, :] + other_ref[early, :]
        for half in range(2):
            rows = slice(half * HALF + 4 * front, half * HALF + 4 * front + 4)
            for piece in range(2):
                at = base + EARLY + half * 8 + piece * 4
                out_ref[at : at + 4, :] = coupled_ref[rows, piece * 128 : piece * 128 + 128]


def total_kernel(pieces_ref, out_ref):
    core = lax.axis_index("core")
    total = pieces_ref[0]
    for index in range(1, FRONT):
        total = total + pieces_ref[index]
    out_ref[...] = jnp.zeros_like(out_ref)
    for zl in range(4):
        out_ref[zl * 2 + core, :S2] = total[zl * PART : zl * PART + S2]
        for other in range(4):
            at = CROSS + NODE * other
            out_ref[zl * 2 + core, at : at + NODE] = total[
                other * PART + S2 : other * PART + S2 + NODE
            ]
        for half in range(2):
            for piece in range(2):
                at = EARLY + half * 8 + piece * 4 + zl
                out_ref[zl * 2 + half, R2V + piece : R2V + piece + 1] = total[at : at + 1]


def share_kernel(pieces_ref, cross_ref, node_ref):
    total = pieces_ref[0]
    for index in range(1, 8):
        total = total + pieces_ref[index]
    for index in range(16):
        cross_ref[index] = total[:CROSS]
    node_ref[...] = total[CROSS:]


def nodes_kernel(cross_ref, node_ref, out_ref):
    zh = lax.axis_index("zh")
    order = [zh, zh ^ 1, zh ^ 2, zh ^ 3]
    for zl in range(4):
        nodes = [cross_ref[node * 4 + zl] for node in order]
        pair, other = nodes[0] + nodes[1], nodes[2] + nodes[3]
        total = pair + other
        spread = jnp.concatenate(
            [node[R2V : R2V + 2] for node in nodes]
            + [node[A2 : A2 + 1] for node in nodes]
            + [value[R1V : R1V + 2] for value in (pair, other)]
            + [value[A1 : A1 + 1] for value in (pair, other)]
            + [total[R0V : R0V + 5], pair[S1 : S1 + 4]]
            + [node_ref[NODE * zl : NODE * zl + NODE], jnp.zeros((1, 128), F32)],
            axis=0,
        )
        for front in range(FRONT):
            out_ref[front, zl * SPREAD : zl * SPREAD + SPREAD] = spread


def solve_kernel(
    rank_ref, mine_ref, other_ref, own_ref, forward_ref, mix_ref, out_hbm,
    out_ref, out_sems,
):
    def solve(low_ref, high_ref):
        stores = []

        def finish(level, value):
            out_ref[level] = value
            copy = pltpu.make_async_copy(out_ref.at[level], out_hbm.at[level], out_sems.at[level])
            copy.start()
            stores.append(copy)

        def block(at):
            rows = pl.ds(at, HALF, stride=SPREAD)
            return jnp.concatenate([low_ref[rows, :], high_ref[rows, :]], axis=0)

        def wide(at):
            return jnp.concatenate([block(at), block(at + 1)], axis=1)

        def mask(coupling, value):
            keep = lax.broadcasted_iota(jnp.int32, value.shape, 0) < rank_ref[:, coupling : coupling + 1]
            return jnp.where(keep, value, 0.0)

        def expand(level, lanes, *values):
            high, low = split(jnp.concatenate(values, axis=0))
            left_high, left_low = mix_ref[level, 0, :, lanes], mix_ref[level, 1, :, lanes]
            return mm(left_high, high) + (mm(left_high, low) + mm(left_low, high))

        def couple(blocks, values):
            left = [block(at) for at in blocks]
            return mm3(jnp.concatenate(left, axis=1), jnp.concatenate(values, axis=0))

        c2 = [mask(2, wide(G_R2V + 2 * node)) for node in range(4)]
        t1 = [
            couple((G_A2 + 2 * half, G_A2 + 2 * half + 1), c2[2 * half : 2 * half + 2])
            for half in range(2)
        ]
        c1 = [mask(1, wide(G_R1V + 2 * half) - t1[half]) for half in range(2)]
        c0 = mask(0, wide(G_R0V) - couple((G_A1, G_A1 + 1), c1))
        d0 = mask(0, wide(G_S0) - couple((G_B0,), (c0,)))
        finish(0, own_ref[0] - expand(0, slice(0, RANK), c0))
        d1 = mask(1, wide(G_S1) - couple((G_B1, G_C1), (c1[0], d0)))
        finish(1, own_ref[1] - expand(1, slice(0, 2 * RANK), c1[0], d0))
        d2 = mask(2, wide(G_S2) - couple((G_B2, G_C2), (c2[0], d1)))
        finish(2, own_ref[2] - expand(2, slice(0, 2 * RANK), c2[0], d1))
        finish(3, forward_ref[...] - expand(3, slice(RANK, 2 * RANK), d2))
        for copy in stores:
            copy.wait()

    core = lax.axis_index("core")
    pl.when(core == 0)(lambda: solve(mine_ref, other_ref))
    pl.when(core == 1)(lambda: solve(other_ref, mine_ref))


def per_device(rhs, dinv, u_factor, v_factor, rank_sizes, resid, dest_front, dest_row, live_count):

    front = ("x", "y")
    swap = [(0, 1), (1, 0)]

    packed = pl.pallas_call(
        pack_kernel,
        out_shape=jax.ShapeDtypeStruct((FRONT * SLOTS, SHOTS + 128), F32),
        in_specs=[HBM] * 4,
        out_specs=VMEM,
        scratch_shapes=[
            pltpu.VMEM((1, 1), jnp.int32),
            pltpu.VMEM(resid.shape, F32),
            pltpu.VMEM((1, resid.shape[0]), jnp.int32),
            pltpu.VMEM((1, resid.shape[0]), jnp.int32),
            pltpu.SemaphoreType.DMA((4,)),
        ],
        compiler_params=params(WHOLE),
    )(live_count.reshape(1, 1), resid, dest_front.reshape(1, -1), dest_row.reshape(1, -1))
    packed, dinv_after = lax.optimization_barrier((packed, dinv))
    got = lax.all_to_all(
        packed.reshape(FRONT, SLOTS, SHOTS + 128), front, 0, 0, tiled=True
    ).reshape(FRONT * SLOTS, SHOTS + 128)

    early = jax.ShapeDtypeStruct((HALF * PART, 128), F32)
    mine, send = pl.pallas_call(
        local_kernel,
        out_shape=(early, early),
        in_specs=[HBM] * 4,
        out_specs=(VMEM, VMEM),
        scratch_shapes=[
            pltpu.VMEM((LEVELS - 1, ROWS, SHOTS), BF16),
            pltpu.VMEM((LEVELS - 1, ROWS, ROWS), BF16),
            pltpu.VMEM((LEVELS - 1, ROWS, RANK), BF16),
            pltpu.VMEM((LEVELS - 2, ROWS, RANK), BF16),
            pltpu.VMEM((RANK, SHOTS), F32),
            pltpu.VMEM((RANK, RANK), F32),
            pltpu.SemaphoreType.DMA((LEVELS - 1, 4)),
        ],
        compiler_params=params(LOCAL),
        cost_estimate=pl.CostEstimate(
            flops=20_000_000_000, bytes_accessed=8_000_000, transcendentals=0
        ),
    )(rhs, dinv_after, u_factor, v_factor)
    other = lax.ppermute(send, "core", swap)

    forward, coupled = pl.pallas_call(
        bottom_kernel,
        out_shape=(
            jax.ShapeDtypeStruct((ROWS, SHOTS), F32),
            jax.ShapeDtypeStruct((RANK, SHOTS), F32),
        ),
        in_specs=[VMEM] * 4,
        out_specs=(VMEM, VMEM),
        compiler_params=params(8),
        cost_estimate=pl.CostEstimate(
            flops=20_000_000_000, bytes_accessed=4_000_000, transcendentals=0
        ),
    )(got, dinv, v_factor, rhs)
    message = pl.pallas_call(
        message_kernel,
        out_shape=jax.ShapeDtypeStruct((FRONT * MESSAGE, 128), F32),
        in_specs=[VMEM] * 3,
        out_specs=VMEM,
        compiler_params=params(4),
    )(coupled, mine, other)

    message, dinv_late = lax.optimization_barrier((message, dinv))
    own, mix = pl.pallas_call(
        fields_kernel,
        out_shape=(
            jax.ShapeDtypeStruct((LEVELS - 1, ROWS, SHOTS), F32),
            jax.ShapeDtypeStruct((LEVELS, 2, ROWS, 2 * RANK), BF16),
        ),
        in_specs=[VMEM] * 4,
        out_specs=(VMEM,) * 2,
        compiler_params=params(8),
        cost_estimate=pl.CostEstimate(
            flops=1_200_000_000, bytes_accessed=5_000_000, transcendentals=0
        ),
    )(rhs, dinv_late, u_factor, v_factor)
    pieces = lax.all_to_all(message.reshape(FRONT, MESSAGE, 128), front, 0, 0, tiled=True)
    summed = pl.pallas_call(
        total_kernel,
        out_shape=jax.ShapeDtypeStruct((8, SENT, 128), F32),
        in_specs=[VMEM],
        out_specs=VMEM,
        compiler_params=params(4),
    )(pieces)
    pieces = lax.all_to_all(summed, ("zl", "core"), 0, 0, tiled=True)
    cross, node = pl.pallas_call(
        share_kernel,
        out_shape=(
            jax.ShapeDtypeStruct((16, CROSS, 128), F32),
            jax.ShapeDtypeStruct((4 * NODE, 128), F32),
        ),
        in_specs=[VMEM],
        out_specs=(VMEM, VMEM),
        compiler_params=params(4),
    )(pieces)
    cross = lax.all_to_all(cross, ("zh", "zl"), 0, 0, tiled=True)
    spread = pl.pallas_call(
        nodes_kernel,
        out_shape=jax.ShapeDtypeStruct((FRONT, 4 * SPREAD, 128), F32),
        in_specs=[VMEM, VMEM],
        out_specs=VMEM,
        compiler_params=params(4),
    )(cross, node)
    gathered = lax.all_to_all(spread, front, 0, 0, tiled=True).reshape(HALF * SPREAD, 128)
    other = lax.ppermute(gathered, "core", swap)

    return pl.pallas_call(
        solve_kernel,
        out_shape=jax.ShapeDtypeStruct((LEVELS, ROWS, SHOTS), F32),
        in_specs=[VMEM] * 6,
        out_specs=HBM,
        scratch_shapes=[
            pltpu.VMEM((LEVELS, ROWS, SHOTS), F32),
            pltpu.SemaphoreType.DMA((LEVELS,)),
        ],
        compiler_params=params(SOLVE),
    )(rank_sizes.reshape(1, -1), gathered, other, own, forward, mix)


def solution(mesh):
    grid = Mesh(mesh.devices.reshape(4, 4, 2, 4, 4), ALL)
    wide = P(None, ALL, None)
    return jax.shard_map(
        per_device,
        mesh=grid,
        in_specs=(wide, wide, wide, wide, P(), P(ALL, None), P(ALL, None), P(ALL), P(ALL)),
        out_specs=wide,
        check_vma=False,
    )
```

```python
import functools

import jax
import jax.numpy as jnp
from jax import lax
from jax.experimental import pallas as pl
from jax.experimental.pallas import tpu as pltpu
from jax.sharding import Mesh
from jax.sharding import PartitionSpec as P

F32 = jnp.float32
BF16 = jnp.bfloat16
LEVELS = 4
RANK = 128
SHOTS = 256
ROWS = 384
SLOTS = 8
FRONT = 16
HALF = RANK // 2
PART = 18
EARLY = 4 * PART
MESSAGE = EARLY + 16
SENT = 32
CROSS = 16
NODE = 4
SPREAD = 32
ALL = ("zh", "zl", "core", "x", "y")

A2, R1V, A1, R0V, S0, B0, S1, B1, C1, S2, B2, C2 = 0, 1, 3, 4, 6, 8, 9, 11, 12, 13, 15, 16
R2V = S2
G_R2V, G_A2, G_R1V, G_A1, G_R0V, G_S0, G_B0, G_S1, G_B1, G_C1, G_S2, G_B2, G_C2 = (
    0, 8, 12, 16, 18, 20, 22, 23, 25, 26, 27, 29, 30,
)


SOLVE = 16
LOCAL = 54
WHOLE = 54


def params(mebibytes):
    return pltpu.CompilerParams(vmem_limit_bytes=int(mebibytes * 2**20))


VMEM = pl.BlockSpec(memory_space=pltpu.VMEM)
HBM = pl.BlockSpec(memory_space=pltpu.HBM)


def split(value):
    high = value.astype(BF16)
    return high, (value - high.astype(F32)).astype(BF16)


def split3(value):
    high = value.astype(BF16)
    rest = value - high.astype(F32)
    mid = rest.astype(BF16)
    return high, mid, (rest - mid.astype(F32)).astype(BF16)


def mm(left, right):
    return jnp.dot(left, right, preferred_element_type=F32)


def mm_tn(left, right):
    return lax.dot_general(left, right, (((0,), (0,)), ((), ())), preferred_element_type=F32)


def mm_nt(left, right):
    return lax.dot_general(left, right, (((1,), (1,)), ((), ())), preferred_element_type=F32)


def mm3(left, right):
    left_high, left_low = split(left)
    right_high, right_low = split(right)
    return mm(left_high, right_high) + (mm(left_high, right_low) + mm(left_low, right_high))


def pack_kernel(
    live_hbm, resid_hbm, front_hbm, row_hbm, out_ref,
    live_ref, resid_ref, front_ref, row_ref, sems,
):
    copies = [
        pltpu.make_async_copy(source, target, sems.at[index])
        for index, (source, target) in enumerate(
            (
                (front_hbm, front_ref),
                (row_hbm, row_ref),
                (resid_hbm, resid_ref),
                (live_hbm, live_ref),
            )
        )
    ]
    for copy in copies:
        copy.start()
    recv = resid_ref.shape[0]
    sublane = lax.broadcasted_iota(jnp.int32, (recv, recv), 0)
    lane = lax.broadcasted_iota(jnp.int32, (recv, recv), 1)
    copies[0].wait()
    front = front_ref[...]
    column = jnp.sum(jnp.where(sublane == lane, front, 0), axis=1, keepdims=True)
    earlier = (column == front) & (sublane < lane)
    slot = front * SLOTS + jnp.sum(earlier.astype(jnp.int32), axis=0, keepdims=True)
    copies[3].wait()
    live = lane[:1] < live_ref[...]
    place = live & (
        lax.broadcasted_iota(jnp.int32, (FRONT * SLOTS, recv), 0) == slot
    )
    copies[1].wait()
    rows = jnp.sum(jnp.where(place, row_ref[...] + 1, 0), axis=1, keepdims=True)
    out_ref[:, SHOTS:] = jnp.broadcast_to(rows.astype(F32), (FRONT * SLOTS, 128))
    place = place.astype(F32).astype(BF16)
    copies[2].wait()
    high, mid, low = split3(resid_ref[...])
    out_ref[:, :SHOTS] = mm(place, high) + (mm(place, mid) + mm(place, low))


def local_kernel(
    rhs_hbm, dinv_hbm, u_hbm, v_hbm, mine_ref, send_ref,
    rhs_ref, dinv_ref, u_ref, v_ref, wide_ref, narrow_ref, sems,
):
    core = lax.axis_index("core")
    loads = []
    for level in range(LEVELS - 1):
        pairs = [
            (dinv_hbm.at[level], dinv_ref.at[level]),
            (rhs_hbm.at[level], rhs_ref.at[level]),
            (u_hbm.at[level], u_ref.at[level]),
        ]
        if level > 0:
            pairs.append((v_hbm.at[level - 1], v_ref.at[level - 1]))
        loads.append(
            [
                pltpu.make_async_copy(source, target, sems.at[level, index])
                for index, (source, target) in enumerate(pairs)
            ]
        )
        for copy in loads[-1]:
            copy.start()

    def save(at, value):
        scratch = narrow_ref if value.shape[1] == 128 else wide_ref
        scratch[...] = value
        for piece in range(value.shape[1] // 128):
            rows = pl.ds(at + piece, HALF, stride=PART)
            lanes = slice(piece * 128, piece * 128 + 128)
            mine_ref[rows, :] = scratch[pl.ds(core * HALF, HALF), lanes]
            send_ref[rows, :] = scratch[pl.ds((1 - core) * HALF, HALF), lanes]

    save(PART - 1, jnp.zeros((RANK, 128), F32))
    for level in range(LEVELS - 1):
        for copy in loads[level]:
            copy.wait()
        block = dinv_ref[level]
        factor = u_ref[level]
        narrow = factor
        if level > 0:
            narrow = jnp.concatenate([factor, v_ref[level - 1]], axis=1)
            factor = narrow
        own = split(mm(block, rhs_ref[level]))
        mix = split(mm(block, narrow))
        own = mm_tn(factor, own[0]) + mm_tn(factor, own[1])
        mix = mm_tn(factor, mix[0]) + mm_tn(factor, mix[1])
        save((S0, S1, S2)[level], own[:RANK])
        save((B0, B1, B2)[level], mix[:RANK, :RANK])
        if level > 0:
            save((None, C1, C2)[level], mix[:RANK, RANK:])
            save((None, R0V, R1V)[level], own[RANK:])
            save((None, A1, A2)[level], mix[RANK:, :RANK])


def fields_kernel(rhs_ref, dinv_ref, u_ref, v_ref, own_ref, mix_ref):
    for level in range(LEVELS):
        block = dinv_ref[level]
        if level < LEVELS - 1:
            own_ref[level] = mm(block, rhs_ref[level])
            for part, value in enumerate(split(mm(block, u_ref[level]))):
                mix_ref[level, part, :, :RANK] = value
        if level > 0:
            for part, value in enumerate(split(mm(block, v_ref[level - 1]))):
                mix_ref[level, part, :, RANK:] = value


def bottom_kernel(got_ref, dinv_ref, v_ref, rhs_ref, forward_ref, coupled_ref):
    rowid = got_ref[:, SHOTS:]
    lane = lax.broadcasted_iota(jnp.int32, rowid.shape, 1).astype(F32) + 1.0
    select = jnp.concatenate(
        [(rowid == lane + 128.0 * part).astype(F32).astype(BF16) for part in range(ROWS // 128)],
        axis=1,
    )
    high, mid, low = split3(got_ref[:, :SHOTS])
    block = dinv_ref[LEVELS - 1]
    chosen = mm_nt(block, select).astype(BF16)
    twice = jnp.concatenate([chosen, chosen], axis=1)
    forward = mm(block, rhs_ref[LEVELS - 1]) + (
        mm(twice, jnp.concatenate([high, mid], axis=0)) + mm(chosen, low)
    )
    forward_ref[...] = forward
    high, low = split(forward)
    factor = v_ref[LEVELS - 2]
    coupled_ref[...] = mm_tn(
        jnp.concatenate([factor, factor], axis=0), jnp.concatenate([high, low], axis=0)
    )


def message_kernel(coupled_ref, mine_ref, other_ref, out_ref):
    for front in range(FRONT):
        early = slice(front * EARLY, front * EARLY + EARLY)
        base = front * MESSAGE
        out_ref[base : base + EARLY, :] = mine_ref[early, :] + other_ref[early, :]
        for half in range(2):
            rows = slice(half * HALF + 4 * front, half * HALF + 4 * front + 4)
            for piece in range(2):
                at = base + EARLY + half * 8 + piece * 4
                out_ref[at : at + 4, :] = coupled_ref[rows, piece * 128 : piece * 128 + 128]


def total_kernel(pieces_ref, out_ref):
    core = lax.axis_index("core")
    total = pieces_ref[0]
    for index in range(1, FRONT):
        total = total + pieces_ref[index]
    out_ref[...] = jnp.zeros_like(out_ref)
    for zl in range(4):
        out_ref[zl * 2 + core, :S2] = total[zl * PART : zl * PART + S2]
        for other in range(4):
            at = CROSS + NODE * other
            out_ref[zl * 2 + core, at : at + NODE] = total[
                other * PART + S2 : other * PART + S2 + NODE
            ]
        for half in range(2):
            for piece in range(2):
                at = EARLY + half * 8 + piece * 4 + zl
                out_ref[zl * 2 + half, R2V + piece : R2V + piece + 1] = total[at : at + 1]


def share_kernel(pieces_ref, cross_ref, node_ref):
    total = pieces_ref[0]
    for index in range(1, 8):
        total = total + pieces_ref[index]
    for index in range(16):
        cross_ref[index] = total[:CROSS]
    node_ref[...] = total[CROSS:]


def nodes_kernel(cross_ref, node_ref, out_ref):
    zh = lax.axis_index("zh")
    order = [zh, zh ^ 1, zh ^ 2, zh ^ 3]
    for zl in range(4):
        nodes = [cross_ref[node * 4 + zl] for node in order]
        pair, other = nodes[0] + nodes[1], nodes[2] + nodes[3]
        total = pair + other
        spread = jnp.concatenate(
            [node[R2V : R2V + 2] for node in nodes]
            + [node[A2 : A2 + 1] for node in nodes]
            + [value[R1V : R1V + 2] for value in (pair, other)]
            + [value[A1 : A1 + 1] for value in (pair, other)]
            + [total[R0V : R0V + 5], pair[S1 : S1 + 4]]
            + [node_ref[NODE * zl : NODE * zl + NODE], jnp.zeros((1, 128), F32)],
            axis=0,
        )
        for front in range(FRONT):
            out_ref[front, zl * SPREAD : zl * SPREAD + SPREAD] = spread


def solve_kernel(
    rank_ref, mine_ref, other_ref, own_ref, forward_ref, mix_ref, out_hbm,
    out_ref, out_sems,
):
    def solve(low_ref, high_ref):
        stores = []

        def finish(level, value):
            out_ref[level] = value
            copy = pltpu.make_async_copy(out_ref.at[level], out_hbm.at[level], out_sems.at[level])
            copy.start()
            stores.append(copy)

        def block(at):
            rows = pl.ds(at, HALF, stride=SPREAD)
            return jnp.concatenate([low_ref[rows, :], high_ref[rows, :]], axis=0)

        def wide(at):
            return jnp.concatenate([block(at), block(at + 1)], axis=1)

        def mask(coupling, value):
            keep = lax.broadcasted_iota(jnp.int32, value.shape, 0) < rank_ref[:, coupling : coupling + 1]
            return jnp.where(keep, value, 0.0)

        def expand(level, lanes, *values):
            high, low = split(jnp.concatenate(values, axis=0))
            left_high, left_low = mix_ref[level, 0, :, lanes], mix_ref[level, 1, :, lanes]
            return mm(left_high, high) + (mm(left_high, low) + mm(left_low, high))

        def couple(blocks, values):
            left = [block(at) for at in blocks]
            return mm3(jnp.concatenate(left, axis=1), jnp.concatenate(values, axis=0))

        c2 = [mask(2, wide(G_R2V + 2 * node)) for node in range(4)]
        t1 = [
            couple((G_A2 + 2 * half, G_A2 + 2 * half + 1), c2[2 * half : 2 * half + 2])
            for half in range(2)
        ]
        c1 = [mask(1, wide(G_R1V + 2 * half) - t1[half]) for half in range(2)]
        c0 = mask(0, wide(G_R0V) - couple((G_A1, G_A1 + 1), c1))
        d0 = mask(0, wide(G_S0) - couple((G_B0,), (c0,)))
        finish(0, own_ref[0] - expand(0, slice(0, RANK), c0))
        d1 = mask(1, wide(G_S1) - couple((G_B1, G_C1), (c1[0], d0)))
        finish(1, own_ref[1] - expand(1, slice(0, 2 * RANK), c1[0], d0))
        d2 = mask(2, wide(G_S2) - couple((G_B2, G_C2), (c2[0], d1)))
        finish(2, own_ref[2] - expand(2, slice(0, 2 * RANK), c2[0], d1))
        finish(3, forward_ref[...] - expand(3, slice(RANK, 2 * RANK), d2))
        for copy in stores:
            copy.wait()

    core = lax.axis_index("core")
    pl.when(core == 0)(lambda: solve(mine_ref, other_ref))
    pl.when(core == 1)(lambda: solve(other_ref, mine_ref))


def per_device(rhs, dinv, u_factor, v_factor, rank_sizes, resid, dest_front, dest_row, live_count):

    front = ("x", "y")
    swap = [(0, 1), (1, 0)]

    packed = pl.pallas_call(
        pack_kernel,
        out_shape=jax.ShapeDtypeStruct((FRONT * SLOTS, SHOTS + 128), F32),
        in_specs=[HBM] * 4,
        out_specs=VMEM,
        scratch_shapes=[
            pltpu.VMEM((1, 1), jnp.int32),
            pltpu.VMEM(resid.shape, F32),
            pltpu.VMEM((1, resid.shape[0]), jnp.int32),
            pltpu.VMEM((1, resid.shape[0]), jnp.int32),
            pltpu.SemaphoreType.DMA((4,)),
        ],
        compiler_params=params(WHOLE),
    )(live_count.reshape(1, 1), resid, dest_front.reshape(1, -1), dest_row.reshape(1, -1))
    packed, dinv_after = lax.optimization_barrier((packed, dinv))
    got = lax.all_to_all(
        packed.reshape(FRONT, SLOTS, SHOTS + 128), front, 0, 0, tiled=True
    ).reshape(FRONT * SLOTS, SHOTS + 128)

    early = jax.ShapeDtypeStruct((HALF * PART, 128), F32)
    mine, send = pl.pallas_call(
        local_kernel,
        out_shape=(early, early),
        in_specs=[HBM] * 4,
        out_specs=(VMEM, VMEM),
        scratch_shapes=[
            pltpu.VMEM((LEVELS - 1, ROWS, SHOTS), BF16),
            pltpu.VMEM((LEVELS - 1, ROWS, ROWS), BF16),
            pltpu.VMEM((LEVELS - 1, ROWS, RANK), BF16),
            pltpu.VMEM((LEVELS - 2, ROWS, RANK), BF16),
            pltpu.VMEM((RANK, SHOTS), F32),
            pltpu.VMEM((RANK, RANK), F32),
            pltpu.SemaphoreType.DMA((LEVELS - 1, 4)),
        ],
        compiler_params=params(LOCAL),
        cost_estimate=pl.CostEstimate(
            flops=20_000_000_000, bytes_accessed=8_000_000, transcendentals=0
        ),
    )(rhs, dinv_after, u_factor, v_factor)
    other = lax.ppermute(send, "core", swap)

    forward, coupled = pl.pallas_call(
        bottom_kernel,
        out_shape=(
            jax.ShapeDtypeStruct((ROWS, SHOTS), F32),
            jax.ShapeDtypeStruct((RANK, SHOTS), F32),
        ),
        in_specs=[VMEM] * 4,
        out_specs=(VMEM, VMEM),
        compiler_params=params(8),
        cost_estimate=pl.CostEstimate(
            flops=20_000_000_000, bytes_accessed=4_000_000, transcendentals=0
        ),
    )(got, dinv, v_factor, rhs)
    message = pl.pallas_call(
        message_kernel,
        out_shape=jax.ShapeDtypeStruct((FRONT * MESSAGE, 128), F32),
        in_specs=[VMEM] * 3,
        out_specs=VMEM,
        compiler_params=params(4),
    )(coupled, mine, other)

    message, dinv_late = lax.optimization_barrier((message, dinv))
    own, mix = pl.pallas_call(
        fields_kernel,
        out_shape=(
            jax.ShapeDtypeStruct((LEVELS - 1, ROWS, SHOTS), F32),
            jax.ShapeDtypeStruct((LEVELS, 2, ROWS, 2 * RANK), BF16),
        ),
        in_specs=[VMEM] * 4,
        out_specs=(VMEM,) * 2,
        compiler_params=params(8),
        cost_estimate=pl.CostEstimate(
            flops=1_200_000_000, bytes_accessed=5_000_000, transcendentals=0
        ),
    )(rhs, dinv_late, u_factor, v_factor)
    pieces = lax.all_to_all(message.reshape(FRONT, MESSAGE, 128), front, 0, 0, tiled=True)
    summed = pl.pallas_call(
        total_kernel,
        out_shape=jax.ShapeDtypeStruct((8, SENT, 128), F32),
        in_specs=[VMEM],
        out_specs=VMEM,
        compiler_params=params(4),
    )(pieces)
    pieces = lax.all_to_all(summed, ("zl", "core"), 0, 0, tiled=True)
    cross, node = pl.pallas_call(
        share_kernel,
        out_shape=(
            jax.ShapeDtypeStruct((16, CROSS, 128), F32),
            jax.ShapeDtypeStruct((4 * NODE, 128), F32),
        ),
        in_specs=[VMEM],
        out_specs=(VMEM, VMEM),
        compiler_params=params(4),
    )(pieces)
    cross = lax.all_to_all(cross, ("zh", "zl"), 0, 0, tiled=True)
    spread = pl.pallas_call(
        nodes_kernel,
        out_shape=jax.ShapeDtypeStruct((FRONT, 4 * SPREAD, 128), F32),
        in_specs=[VMEM, VMEM],
        out_specs=VMEM,
        compiler_params=params(4),
    )(cross, node)
    gathered = lax.all_to_all(spread, front, 0, 0, tiled=True).reshape(HALF * SPREAD, 128)
    other = lax.ppermute(gathered, "core", swap)

    return pl.pallas_call(
        solve_kernel,
        out_shape=jax.ShapeDtypeStruct((LEVELS, ROWS, SHOTS), F32),
        in_specs=[VMEM] * 6,
        out_specs=HBM,
        scratch_shapes=[
            pltpu.VMEM((LEVELS, ROWS, SHOTS), F32),
            pltpu.SemaphoreType.DMA((LEVELS,)),
        ],
        compiler_params=params(SOLVE),
    )(rank_sizes.reshape(1, -1), gathered, other, own, forward, mix)


def solution(mesh):
    grid = Mesh(mesh.devices.reshape(4, 4, 2, 4, 4), ALL)
    wide = P(None, ALL, None)
    return jax.shard_map(
        per_device,
        mesh=grid,
        in_specs=(wide, wide, wide, wide, P(), P(ALL, None), P(ALL, None), P(ALL), P(ALL)),
        out_specs=wide,
        check_vma=False,
    )
```
